128 devices in a mesh: dx: 16 (over z, y), dy: 8 (over x, core).
Axes of the slice: x: 4, y: 4, z: 4, core: 2. Of those that a mesh axis runs over, the one named last changes fastest.
Arguments:
- charges: bfloat16 [8192, 128, 128], P(('dx', 'dy')), may hold values from -6 to 6
- basis: bfloat16 [8192, 81, 128], P(('dx', 'dy')), may hold values from -0.5 to 0.5
- leaf_count: int32 [8192], P(('dx', 'dy')), may hold values from 64 to 128, as said below
- cotangent: bfloat16 [8192, 128, 128], P(('dx', 'dy')), may hold values from -6 to 6
- m2l_ops: bfloat16 [316, 81, 81], replicated, may hold values from -0.3125 to 0.3125
- fetch_cells: int32 [128, 128, 1], P(('dx', 'dy')), may hold values from 0 to 63
- pair_target: int32 [128, 16, 32], P(('dx', 'dy')), may hold values from 0 to 63
- pair_source: int32 [128, 16, 32], P(('dx', 'dy')), may hold values from 0 to 191
- batch_class: int32 [128, 16], P(('dx', 'dy')), may hold values from 0 to 315
- batch_fill: int32 [128, 16], P(('dx', 'dy')), may hold values from 0 to 32, as said below
Outputs:
- potential: bfloat16 [8192, 128, 128], P(('dx', 'dy'))
- charge_grad: bfloat16 [8192, 128, 128], P(('dx', 'dy'))
The draws below stay inside these ranges and needn't reach their ends.
Inputs may be any that keep to these rules, and one draw needn't show every extreme that they name: `leaf_count`: in every draw some leaf is full. `batch_fill`: in each domain the batches with a positive count come first, 4 of them or more; the first batch of every domain is full, and on some domain all batches are live.
All inputs are finite; a program needn't handle non-finite values.
Results may differ from the reference program's by a relative error of at most 0.015.
Values may be sent and summed in bfloat16 or wider, within the bound.
No kernel may reach another device: no remote copies, remote signals or barrier semaphores. Data moves between devices by JAX's collectives and lax.ppermute only.
A program may use at most 128 MiB of HBM per device.

```python
import jax
import jax.numpy as jnp
from jax import lax

K = 81
C = 128
NCLASS = 316
CELLS_DEV = 64
SLOTS = 128
CAP = 1
NBATCH = 16
BATCH = 32
DOMAINS = 128
CELLS = 8192
SOURCES = 192
N_DX = 16
N_DY = 8


def draw_leaf_count(key, part):
    key = jax.random.fold_in(key, 5)
    key_counts, key_full = jax.random.split(key)
    counts = jax.random.randint(key_counts, (CELLS,), SLOTS // 2, SLOTS + 1)
    full_cell = jax.random.randint(key_full, (), 0, CELLS)
    return jnp.where(jnp.arange(CELLS) == full_cell, SLOTS, counts).astype(jnp.int32)


def draw_batch_fill(key, part):
    key = jax.random.fold_in(key, 11)
    key_rolls, key_heavy, key_fills = jax.random.split(key, 3)
    rolled = jax.random.randint(key_rolls, (DOMAINS,), 0, 64)
    heavy_domain = jax.random.randint(key_heavy, (), 0, DOMAINS)
    rolled = jnp.where(jnp.arange(DOMAINS) == heavy_domain, 63, rolled)
    quarter = NBATCH // 4
    live_batches = quarter + rolled * rolled * rolled * (NBATCH - quarter) // (63 * 63 * 63)
    fills = jax.random.randint(key_fills, (DOMAINS, NBATCH), BATCH // 2, BATCH + 1)
    fills = fills.at[:, 0].set(BATCH)
    positions = jnp.arange(NBATCH)[None, :]
    return jnp.where(positions < live_batches[:, None], fills, 0).astype(jnp.int32)


def place_ends(entries, rng, low, high):
    spot = [jax.random.randint(jax.random.fold_in(rng, axis), (), 0, length) for axis, length in enumerate(entries.shape)]
    main_axis = entries.shape.index(max(entries.shape))
    beside = spot[:main_axis] + [(spot[main_axis] + 1) % entries.shape[main_axis]] + spot[main_axis + 1:]
    return entries.at[tuple(spot)].set(low).at[tuple(beside)].set(high)


def block_scale(own_key, extent, cuts, least, largest):
    factor_of, own = 1.0, jax.random.fold_in(own_key, 6)
    for dim, blocks in cuts:
        heights = jnp.exp(jax.random.uniform(jax.random.fold_in(own, dim), (blocks,), jnp.float32, least / len(cuts), largest / len(cuts)))
        factor_of = factor_of * jnp.repeat(heights, extent[dim] // blocks).reshape([-1 if axis == dim else 1 for axis in range(len(extent))])
    return factor_of


def noise(key, extent, width, bound, cuts=(), kind=jnp.bfloat16):
    values = width * jax.random.normal(key, extent, jnp.float32)
    if cuts:
        values = values * block_scale(key, extent, cuts, -0.22, 0.18)
    return jnp.clip(values, -bound, bound).astype(kind)


def setup_inputs(seed: int = 0) -> dict:
    splits = jax.random.split(jax.random.key(seed), 11)
    return {
        "charges": noise(splits[0], (CELLS, SLOTS, C), 1.0, 6.0, ((0, 128),)),
        "basis": noise(splits[1], (CELLS, K, SLOTS), SLOTS ** -0.5, 0.5, ((0, 128),)),
        "leaf_count": draw_leaf_count(jax.random.fold_in(splits[10], 71), 0),
        "cotangent": noise(splits[3], (CELLS, SLOTS, C), 1.0, 6.0, ((0, 128),)),
        "m2l_ops": noise(splits[4], (NCLASS, K, K), (K * NBATCH * BATCH // (2 * CELLS_DEV)) ** -0.5, 0.3125),
        "fetch_cells": place_ends(jax.random.randint(splits[5], (DOMAINS, DOMAINS, CAP), 0, CELLS_DEV), jax.random.fold_in(splits[5], 1), 0, CELLS_DEV - 1).astype(jnp.int32),
        "pair_target": place_ends(jax.random.randint(splits[6], (DOMAINS, NBATCH, BATCH), 0, CELLS_DEV), jax.random.fold_in(splits[6], 1), 0, CELLS_DEV - 1).astype(jnp.int32),
        "pair_source": place_ends(jax.random.randint(splits[7], (DOMAINS, NBATCH, BATCH), 0, CELLS_DEV + N_DX * N_DY * CAP), jax.random.fold_in(splits[7], 1), 0, (CELLS_DEV + N_DX * N_DY * CAP) - 1).astype(jnp.int32),
        "batch_class": place_ends(jax.random.randint(splits[8], (DOMAINS, NBATCH), 0, NCLASS), jax.random.fold_in(splits[8], 1), 0, NCLASS - 1).astype(jnp.int32),
        "batch_fill": draw_batch_fill(jax.random.fold_in(splits[10], 71), 0),
    }


def slot_mask(leaf_count):
    return lax.broadcasted_iota(jnp.int32, (leaf_count.shape[0], SLOTS), 1) < leaf_count[:, None]


def to_moments(basis, values, occupied):
    masked = jnp.where(occupied[:, :, None], values.astype(jnp.float32), jnp.zeros((), jnp.float32))
    return jnp.einsum('iks,isc->ikc', basis.astype(jnp.float32), masked).astype(jnp.bfloat16)


def to_atoms(basis, moments, occupied):
    result = jnp.einsum('iks,ikc->isc', basis.astype(jnp.float32), moments.astype(jnp.float32))
    return jnp.where(occupied[:, :, None], result, jnp.zeros((), jnp.float32)).astype(jnp.bfloat16)


def reference(charges, basis, leaf_count, cotangent, m2l_ops, fetch_cells, pair_target, pair_source, batch_class, batch_fill):
    occupied = slot_mask(leaf_count)
    multipole = to_moments(basis, charges, occupied)
    exp_grad = to_moments(basis, cotangent, occupied)
    operators = m2l_ops.astype(jnp.float32)
    own_cells = jnp.arange(CELLS_DEV, dtype=jnp.int32)
    peer_base = (jnp.arange(DOMAINS, dtype=jnp.int32) * CELLS_DEV)[:, None]
    slot_index = jnp.arange(BATCH, dtype=jnp.int32)

    def one_domain(grad_sum, domain):
        first_cell = domain * CELLS_DEV
        source_cells = jnp.concatenate([first_cell + own_cells, (peer_base + fetch_cells[domain]).reshape(-1).astype(jnp.int32)])
        sources = multipole[source_cells].astype(jnp.float32)
        active = (slot_index[None, :] < batch_fill[domain][:, None])[:, :, None, None]
        chosen = operators[batch_class[domain]]
        picked = jnp.where(active, sources[pair_source[domain]], jnp.zeros((), jnp.float32))
        products = jnp.einsum('bkl,bplc->bpkc', chosen, picked)
        local_exp = jnp.zeros((CELLS_DEV, K, C), jnp.float32).at[pair_target[domain].reshape(-1)].add(products.reshape(-1, K, C))
        own_grads = lax.dynamic_slice_in_dim(exp_grad, first_cell, CELLS_DEV, 0).astype(jnp.float32)
        gathered = jnp.where(active, own_grads[pair_target[domain]], jnp.zeros((), jnp.float32))
        back_products = jnp.einsum('blk,bplc->bpkc', chosen, gathered)
        source_grad = jnp.zeros((SOURCES, K, C), jnp.float32).at[pair_source[domain].reshape(-1)].add(back_products.reshape(-1, K, C))
        remote_part = lax.optimization_barrier(source_grad[CELLS_DEV:].astype(jnp.bfloat16)).astype(jnp.float32)
        combined = jnp.concatenate([source_grad[:CELLS_DEV], remote_part])
        grad_sum = grad_sum.at[source_cells].add(combined)
        return grad_sum, local_exp.astype(jnp.bfloat16)

    grad_sum, local_exp = lax.scan(one_domain, jnp.zeros((CELLS, K, C), jnp.float32), jnp.arange(DOMAINS, dtype=jnp.int32))
    potential = to_atoms(basis, local_exp.reshape(CELLS, K, C), occupied)
    charge_grad = to_atoms(basis, grad_sum.astype(jnp.bfloat16), occupied)
    return potential, charge_grad
```

```python
import jax
import jax.numpy as jnp
from jax import lax
from jax.experimental import pallas as pl
from jax.experimental.pallas import tpu as pltpu
from jax.sharding import PartitionSpec as P

BF = jnp.bfloat16
F32 = jnp.float32
ROWS = 88
MAIN = 80
PACK = 168
CHUNK = 8


def dot(a, b):
    return lax.dot_general(a, b, (((1,), (0,)), ((), ())), preferred_element_type=F32)


def params(mib):
    return pltpu.CompilerParams(vmem_limit_bytes=mib << 20)


def spread_basis(basis_ref, wide_ref, coeffs, cells):
    def put(k, carry):
        wide_ref[pl.ds(pl.multiple_of(k * cells, cells), cells), :] = basis_ref[k].astype(F32)
        return carry

    lax.fori_loop(0, coeffs, put, 0, unroll=9)
    wide_ref[coeffs * cells : (coeffs + 1) * cells, :] = basis_ref[coeffs - 1].astype(F32)
    rest = ROWS - coeffs - 1
    wide_ref[(coeffs + 1) * cells :, :] = jnp.zeros((rest * cells, wide_ref.shape[1]), F32)


def masked_basis(wide_ref, count_ref, cell, cells):
    tile = wide_ref[pl.ds(cell, ROWS, stride=cells), :]
    lane = lax.broadcasted_iota(jnp.int32, tile.shape, 1)
    return jnp.where(lane < count_ref[cell], tile, 0.0)


def first_kernel(
    count_ref,
    target_ref,
    source_ref,
    fill_ref,
    charges_hbm,
    cotangent_hbm,
    basis_hbm,
    chosen_ref,
    mult_ref,
    back_ref,
    own_hbm,
    forward_op_ref,
    charges_ref,
    cotangent_ref,
    basis_ref,
    wide_ref,
    grad_ref,
    total_ref,
    back_op_ref,
    sems,
):
    cells = charges_ref.shape[0]
    coeffs = basis_ref.shape[0]
    batches = chosen_ref.shape[0]
    remote = back_ref.shape[0]
    parts = 4
    step = cells // parts
    basis_copy = pltpu.make_async_copy(basis_hbm, basis_ref, sems.at[0])
    basis_copy.start()
    copies = []
    for part in range(parts):
        rows = pl.ds(part * step, step)
        pair = (
            pltpu.make_async_copy(cotangent_hbm.at[rows], cotangent_ref.at[rows], sems.at[1 + 2 * part]),
            pltpu.make_async_copy(charges_hbm.at[rows], charges_ref.at[rows], sems.at[2 + 2 * part]),
        )
        for copy in pair:
            copy.start()
        copies.append(pair)

    lane = lax.broadcasted_iota(jnp.int32, (ROWS, 128), 1)

    def prepare(b, carry):
        square = chosen_ref[b].astype(F32)
        wide = jnp.pad(square, ((0, 128 - coeffs), (0, 128 - coeffs)))
        back_op_ref[b] = wide.T[:ROWS].astype(BF)
        top = wide[:ROWS]
        moved = pltpu.roll(top, 1, 1)
        forward_op_ref[b] = jnp.where(lane < MAIN, top, jnp.where(lane == MAIN + 1, moved, 0.0)).astype(BF)
        return carry

    lax.fori_loop(0, batches, prepare, 0)

    def clear(e, carry):
        total_ref[e] = jnp.zeros((ROWS, 128), F32)
        return carry

    lax.fori_loop(0, total_ref.shape[0], clear, 0, unroll=4)

    basis_copy.wait()
    spread_basis(basis_ref, wide_ref, coeffs, cells)

    def moment(i, carry):
        tile = masked_basis(wide_ref, count_ref, i, cells).astype(BF)
        both = jnp.concatenate([cotangent_ref[i], charges_ref[i]], axis=1)
        result = dot(tile, both).astype(BF)
        grad_ref[i] = result[:, :128]
        mult_ref[i] = result[:, 128:]
        return carry

    for part in range(parts):
        for copy in copies[part]:
            copy.wait()
        lax.fori_loop(part * step, (part + 1) * step, moment, 0, unroll=4)

    spare = total_ref.shape[0] - 1

    def batch(b, carry):
        fill = fill_ref[b]
        op = back_op_ref[b][:, :ROWS]

        def chunk(j, inner):
            first = j * CHUNK
            for q in range(0, CHUNK, 2):
                p = first + q
                left = grad_ref[target_ref[b, p]]
                right = grad_ref[target_ref[b, p + 1]]
                result = dot(op, jnp.concatenate([left, right], axis=1))
                e0 = jnp.where(p < fill, source_ref[b, p], spare)
                total_ref[e0] += result[:, :128]
                e1 = jnp.where(p + 1 < fill, source_ref[b, p + 1], spare)
                total_ref[e1] += result[:, 128:]
            return inner

        lax.fori_loop(0, (fill + CHUNK - 1) // CHUNK, chunk, 0)
        return carry

    lax.fori_loop(0, batches, batch, 0)
    own_copy = pltpu.make_async_copy(total_ref.at[pl.ds(0, cells)], own_hbm, sems.at[0])
    own_copy.start()

    def narrow(s, carry):
        back_ref[s] = total_ref[cells + s].astype(BF)
        return carry

    lax.fori_loop(0, remote, narrow, 0, unroll=4)
    own_copy.wait()


def pack_kernel(asked_ref, mult_ref, back_ref, out_ref):
    per_step = out_ref.shape[0]
    first = pl.program_id(0) * per_step
    row = lax.broadcasted_iota(jnp.int32, (8, 128), 0)

    def one(s, carry):
        cell = asked_ref[first + s, 0, 0]
        out_ref[s, :MAIN, :] = mult_ref[cell, :MAIN, :]
        out_ref[s, MAIN : 2 * MAIN, :] = back_ref[s, :MAIN, :]
        tail = jnp.where(
            row == 1, mult_ref[cell, MAIN:ROWS, :].astype(F32), back_ref[s, MAIN:ROWS, :].astype(F32)
        )
        out_ref[s, 2 * MAIN : PACK, :] = tail.astype(BF)
        return carry

    lax.fori_loop(0, per_step, one, 0, unroll=4)


def beside_kernel(
    count_ref,
    target_ref,
    source_ref,
    fill_ref,
    mult_ref,
    basis_ref,
    op_ref,
    local_ref,
    atoms_ref,
    number_ref,
    list_batch_ref,
    list_target_ref,
    list_source_ref,
    wide_ref,
    own_target,
    own_source,
):
    cells = mult_ref.shape[0]
    coeffs = basis_ref.shape[0]
    batches = op_ref.shape[0]

    def clear(i, carry):
        local_ref[i] = jnp.zeros((ROWS, 128), F32)
        return carry

    lax.fori_loop(0, cells + 1, clear, 0)
    spread_basis(basis_ref, wide_ref, coeffs, cells)

    def turn(i, carry):
        tile = masked_basis(wide_ref, count_ref, i, cells)
        full = jnp.pad(tile, ((0, 128 - ROWS), (0, 0)))
        atoms_ref[i] = full.T.astype(BF)
        return carry

    lax.fori_loop(0, cells, turn, 0, unroll=2)

    def batch(b, chunks):
        fill = fill_ref[b]
        base = chunks * CHUNK

        def sort(p, counts):
            own, far = counts
            source = source_ref[b, p]
            target = target_ref[b, p]
            is_own = source < cells

            @pl.when(is_own)
            def _():
                own_target[own] = target
                own_source[own] = source

            @pl.when(jnp.logical_not(is_own))
            def _():
                list_target_ref[base + far] = target
                list_source_ref[base + far] = source - cells

            step = is_own.astype(jnp.int32)
            return own + step, far + 1 - step

        own, far = lax.fori_loop(0, fill, sort, (0, 0))
        for q in range(CHUNK):
            own_target[own + q] = cells
            own_source[own + q] = 0
            list_target_ref[base + far + q] = cells
            list_source_ref[base + far + q] = 0
        far_chunks = (far + CHUNK - 1) // CHUNK

        def mark(j, carry):
            list_batch_ref[chunks + j] = b
            return carry

        lax.fori_loop(0, far_chunks, mark, 0)
        op = op_ref[b][:, :ROWS]

        def chunk(j, carry):
            for q in range(0, CHUNK, 2):
                p = j * CHUNK + q
                both = jnp.concatenate([mult_ref[own_source[p]], mult_ref[own_source[p + 1]]], axis=1)
                result = dot(op, both)
                local_ref[own_target[p]] += result[:, :128]
                local_ref[own_target[p + 1]] += result[:, 128:]
            return carry

        lax.fori_loop(0, (own + CHUNK - 1) // CHUNK, chunk, 0)
        return chunks + far_chunks

    number_ref[0] = lax.fori_loop(0, batches, batch, 0)


def last_kernel(
    asked_ref,
    number_ref,
    list_batch_ref,
    list_target_ref,
    list_source_ref,
    incoming_hbm,
    own_hbm,
    local_hbm,
    atoms_hbm,
    op_ref,
    potential_hbm,
    charge_hbm,
    incoming_ref,
    own_ref,
    local_ref,
    atoms_ref,
    potential_ref,
    charge_ref,
    sems,
    out_sems,
):
    cells = own_ref.shape[0]
    remote = incoming_ref.shape[0]
    parts = 4
    step = remote // parts
    own_copy = pltpu.make_async_copy(own_hbm, own_ref, sems.at[0])
    own_copy.start()
    copies = []
    for part in range(parts):
        rows = pl.ds(part * step, step)
        copy = pltpu.make_async_copy(incoming_hbm.at[rows], incoming_ref.at[rows], sems.at[1 + part])
        copy.start()
        copies.append(copy)
    local_copy = pltpu.make_async_copy(local_hbm, local_ref, sems.at[parts + 1])
    local_copy.start()
    atoms_copy = pltpu.make_async_copy(atoms_hbm, atoms_ref, sems.at[parts + 2])
    atoms_copy.start()
    own_copy.wait()

    def collect(s, carry):
        own_ref[asked_ref[s, 0, 0]] += incoming_ref[s, MAIN:PACK, :].astype(F32)
        return carry

    for part in range(parts):
        copies[part].wait()
        lax.fori_loop(part * step, (part + 1) * step, collect, 0, unroll=4)
    local_copy.wait()

    def pick(e):
        return jnp.concatenate([incoming_ref[e, :MAIN, :], incoming_ref[e, 2 * MAIN : PACK, :]], axis=0)

    def chunk(j, carry):
        op = op_ref[list_batch_ref[j]][:, :ROWS]
        for q in range(0, CHUNK, 2):
            p = j * CHUNK + q
            both = jnp.concatenate([pick(list_source_ref[p]), pick(list_source_ref[p + 1])], axis=1)
            result = dot(op, both)
            local_ref[list_target_ref[p]] += result[:, :128]
            local_ref[list_target_ref[p + 1]] += result[:, 128:]
        return carry

    lax.fori_loop(0, number_ref[0], chunk, 0)
    atoms_copy.wait()
    row = lax.broadcasted_iota(jnp.int32, (ROWS, 128), 0)

    def atoms(i, carry):
        grads = jnp.where(row == MAIN + 1, 0.0, own_ref[i]).astype(BF)
        both = jnp.concatenate([local_ref[i].astype(BF), grads], axis=1)
        result = dot(atoms_ref[i][:, :ROWS], both).astype(BF)
        potential_ref[i] = result[:, :128]
        charge_ref[i] = result[:, 128:]
        return carry

    outs = []
    width = cells // parts
    for part in range(parts):
        lax.fori_loop(part * width, (part + 1) * width, atoms, 0, unroll=4)
        rows = pl.ds(part * width, width)
        for place, (ref, hbm) in enumerate(((potential_ref, potential_hbm), (charge_ref, charge_hbm))):
            copy = pltpu.make_async_copy(ref.at[rows], hbm.at[rows], out_sems.at[2 * part + place])
            copy.start()
            outs.append(copy)
    for copy in outs:
        copy.wait()


SMEM = pl.BlockSpec(memory_space=pltpu.SMEM)
VMEM = pl.BlockSpec(memory_space=pltpu.VMEM)
ANY = pl.BlockSpec(memory_space=pl.ANY)


def local(
    charges,
    basis,
    leaf_count,
    cotangent,
    m2l_ops,
    fetch_cells,
    pair_target,
    pair_source,
    batch_class,
    batch_fill,
):
    cells, coeffs, slots = basis.shape
    channels = charges.shape[2]
    domains = fetch_cells.shape[1]
    _, batches, batch_size = pair_target.shape
    classes = m2l_ops.shape[0]
    Shape = jax.ShapeDtypeStruct
    asked = lax.all_to_all(
        fetch_cells.reshape(domains, 1, 1), ("dx", "dy"), split_axis=0, concat_axis=0, tiled=True
    )
    basis_major = basis.transpose(1, 0, 2)
    hot = (batch_class[0][:, None] == lax.broadcasted_iota(jnp.int32, (1, classes), 1)).astype(BF)
    chosen = jnp.einsum("bn,nkl->bkl", hot, m2l_ops, preferred_element_type=F32).astype(BF)
    targets, sources, fill = pair_target[0], pair_source[0], batch_fill[0]
    mult, back, own, forward_ops = pl.pallas_call(
        first_kernel,
        out_shape=(
            Shape((cells, ROWS, channels), BF),
            Shape((domains, ROWS, channels), BF),
            Shape((cells, ROWS, channels), F32),
            Shape((batches, ROWS, 128), BF),
        ),
        in_specs=[SMEM] * 4 + [ANY] * 3 + [VMEM],
        out_specs=(VMEM, VMEM, ANY, VMEM),
        scratch_shapes=[
            pltpu.VMEM((cells, slots, channels), BF),
            pltpu.VMEM((cells, slots, channels), BF),
            pltpu.VMEM((coeffs, cells, slots), BF),
            pltpu.VMEM((ROWS * cells, slots), F32),
            pltpu.VMEM((cells, ROWS, channels), BF),
            pltpu.VMEM((cells + domains + 1, ROWS, channels), F32),
            pltpu.VMEM((batches, ROWS, 128), BF),
            pltpu.SemaphoreType.DMA((9,)),
        ],
        compiler_params=params(48),
        name="moments_back_pairs",
    )(leaf_count, targets, sources, fill, charges, cotangent, basis_major, chosen)
    per_step = 16
    outgoing = pl.pallas_call(
        pack_kernel,
        out_shape=Shape((domains, PACK, channels), BF),
        grid=(domains // per_step,),
        in_specs=[
            SMEM,
            pl.BlockSpec((cells, ROWS, channels), lambda i: (0, 0, 0)),
            pl.BlockSpec((per_step, ROWS, channels), lambda i: (i, 0, 0)),
        ],
        out_specs=pl.BlockSpec((per_step, PACK, channels), lambda i: (i, 0, 0)),
        compiler_params=params(32),
        name="pack_blocks",
    )(asked, mult, back)
    incoming = lax.all_to_all(outgoing, ("dx", "dy"), split_axis=0, concat_axis=0, tiled=True)
    slots_listed = batches * (batch_size + CHUNK)
    local_part, atoms, number, list_batch, list_target, list_source = pl.pallas_call(
        beside_kernel,
        out_shape=(
            Shape((cells + 1, ROWS, channels), F32),
            Shape((cells, slots, 128), BF),
            Shape((1,), jnp.int32),
            Shape((slots_listed // CHUNK,), jnp.int32),
            Shape((slots_listed,), jnp.int32),
            Shape((slots_listed,), jnp.int32),
        ),
        in_specs=[SMEM] * 4 + [VMEM] * 3,
        out_specs=(VMEM, VMEM, SMEM, SMEM, SMEM, SMEM),
        scratch_shapes=[
            pltpu.VMEM((ROWS * cells, slots), F32),
            pltpu.SMEM((batch_size + CHUNK,), jnp.int32),
            pltpu.SMEM((batch_size + CHUNK,), jnp.int32),
        ],
        compiler_params=params(32),
        cost_estimate=pl.CostEstimate(flops=400_000_000, bytes_accessed=8_000_000, transcendentals=0),
        name="own_pairs",
    )(leaf_count, targets, sources, fill, mult, basis_major, forward_ops)
    return pl.pallas_call(
        last_kernel,
        out_shape=(Shape((cells, slots, channels), BF), Shape((cells, slots, channels), BF)),
        in_specs=[SMEM] * 5 + [ANY] * 4 + [VMEM],
        out_specs=(ANY, ANY),
        scratch_shapes=[
            pltpu.VMEM((domains, PACK, channels), BF),
            pltpu.VMEM((cells, ROWS, channels), F32),
            pltpu.VMEM((cells + 1, ROWS, channels), F32),
            pltpu.VMEM((cells, slots, 128), BF),
            pltpu.VMEM((cells, slots, channels), BF),
            pltpu.VMEM((cells, slots, channels), BF),
            pltpu.SemaphoreType.DMA((8,)),
            pltpu.SemaphoreType.DMA((8,)),
        ],
        compiler_params=params(48),
        name="far_pairs_atoms",
    )(asked, number, list_batch, list_target, list_source, incoming, own, local_part, atoms, forward_ops)


def solution(mesh):
    in_specs = (
        P(("dx", "dy"), None, None),
        P(("dx", "dy"), None, None),
        P(("dx", "dy")),
        P(("dx", "dy"), None, None),
        P(),
        P(("dx", "dy"), None, None),
        P(("dx", "dy"), None, None),
        P(("dx", "dy"), None, None),
        P(("dx", "dy"), None),
        P(("dx", "dy"), None),
    )
    out_specs = (P(("dx", "dy"), None, None), P(("dx", "dy"), None, None))
    return jax.shard_map(local, mesh=mesh, in_specs=in_specs, out_specs=out_specs, check_vma=False)
```

```python
import jax
import jax.numpy as jnp
from jax import lax
from jax.experimental import pallas as pl
from jax.experimental.pallas import tpu as pltpu
from jax.sharding import PartitionSpec as P

BF = jnp.bfloat16
F32 = jnp.float32
I32 = jnp.int32
ROWS = 88
MAIN = 80
UNROLL = 16
LIMIT = 62


def dot(a, b):
    return lax.dot_general(a, b, (((1,), (0,)), ((), ())), preferred_element_type=F32)


def params(mib):
    return pltpu.CompilerParams(vmem_limit_bytes=mib << 20)


def spread_basis(basis_ref, wide_ref):
    coeffs, cells, slots = basis_ref.shape

    def put(k, carry):
        wide_ref[pl.ds(pl.multiple_of(k * cells, cells), cells), :] = basis_ref[k].astype(F32)
        return carry

    lax.fori_loop(0, coeffs, put, 0, unroll=9)
    wide_ref[coeffs * cells :, :] = jnp.zeros(((ROWS - coeffs) * cells, slots), F32)


def masked_basis(wide_ref, count_ref, cell, cells):
    tile = wide_ref[pl.ds(cell, ROWS, stride=cells), :]
    lane = lax.broadcasted_iota(I32, tile.shape, 1)
    return jnp.where(lane < count_ref[cell], tile, 0.0)


def clear(ref, count):
    def one(e, carry):
        ref[e] = jnp.zeros(ref.shape[1:], ref.dtype)
        return carry

    lax.fori_loop(0, count, one, 0, unroll=8)


def list_doubles(fill_ref, list_ref, batches):
    def batch(b, count):
        fill = fill_ref[b]

        def double(j, carry):
            live = jnp.where(2 * j + 1 < fill, 3 << 16, 1 << 16)
            list_ref[count + j] = live + b * 64 + 2 * j
            return carry

        doubles = (fill + 1) // 2
        lax.fori_loop(0, doubles, double, 0)
        return count + doubles

    count = lax.fori_loop(0, batches, batch, 0)
    for q in range(UNROLL):
        list_ref[count + q] = 0
    return (count + UNROLL - 1) // UNROLL


def back_kernel(
    count_ref,
    target_ref,
    source_ref,
    fill_ref,
    fetch_ref,
    cotangent_hbm,
    basis_hbm,
    chosen_ref,
    back_hbm,
    own_hbm,
    forward_op_ref,
    cotangent_ref,
    basis_ref,
    wide_ref,
    grad_ref,
    total_ref,
    back_ref,
    back_op_ref,
    list_ref,
    sems,
    out_sems,
):
    cells = cotangent_ref.shape[0]
    coeffs = basis_ref.shape[0]
    batches = chosen_ref.shape[0]
    remote = back_ref.shape[0]
    parts = 4
    step = cells // parts
    basis_copy = pltpu.make_async_copy(basis_hbm, basis_ref, sems.at[0])
    basis_copy.start()
    copies = []
    for part in range(parts):
        rows = pl.ds(part * step, step)
        copy = pltpu.make_async_copy(cotangent_hbm.at[rows], cotangent_ref.at[rows], sems.at[1 + part])
        copy.start()
        copies.append(copy)

    lane = lax.broadcasted_iota(I32, (ROWS, 128), 1)

    def prepare(b, carry):
        square = chosen_ref[b].astype(F32)
        wide = jnp.pad(square, ((0, 128 - coeffs), (0, 128 - coeffs)))
        back_op_ref[b] = wide.T[:ROWS].astype(BF)
        forward_op_ref[b] = wide[:ROWS].astype(BF)
        return carry

    lax.fori_loop(0, batches, prepare, 0, unroll=2)
    turns = list_doubles(fill_ref, list_ref, batches)
    clear(total_ref, cells + remote)
    basis_copy.wait()
    spread_basis(basis_ref, wide_ref)

    def moment(i, carry):
        tile = masked_basis(wide_ref, count_ref, i, cells).astype(BF)
        grad_ref[i] = dot(tile, cotangent_ref[i]).astype(BF)
        return carry

    for part in range(parts):
        copies[part].wait()
        lax.fori_loop(part * step, (part + 1) * step, moment, 0, unroll=8)

    spare = total_ref.shape[0] - 1

    def turn(j, carry):
        for q in range(UNROLL):
            entry = list_ref[j * UNROLL + q]
            b = (entry & 0xFFFF) >> 6
            p = entry & 63
            both = jnp.concatenate([grad_ref[target_ref[b, p]], grad_ref[target_ref[b, p + 1]]], axis=1)
            result = dot(back_op_ref[b][:, :ROWS], both)
            e0 = jnp.where((entry & (1 << 16)) != 0, source_ref[b, p], spare)
            total_ref[e0] += result[:, :128]
            e1 = jnp.where((entry & (1 << 17)) != 0, source_ref[b, p + 1], spare)
            total_ref[e1] += result[:, 128:]
        return carry

    lax.fori_loop(0, turns, turn, 0)
    own_copy = pltpu.make_async_copy(total_ref.at[pl.ds(0, cells)], own_hbm, sems.at[0])
    own_copy.start()
    row = lax.broadcasted_iota(I32, (ROWS - MAIN, 128), 0)

    def narrow(s, carry):
        back_ref[s, :MAIN, :] = total_ref[cells + s, :MAIN, :].astype(BF)
        wish = fetch_ref[0, s].astype(F32)
        back_ref[s, MAIN:, :] = jnp.where(row == 1, wish, total_ref[cells + s, MAIN:, :]).astype(BF)
        return carry

    outs = []
    width = remote // parts
    for part in range(parts):
        lax.fori_loop(part * width, (part + 1) * width, narrow, 0, unroll=8)
        rows = pl.ds(part * width, width)
        copy = pltpu.make_async_copy(back_ref.at[rows], back_hbm.at[rows], out_sems.at[part])
        copy.start()
        outs.append(copy)
    for copy in outs:
        copy.wait()
    own_copy.wait()


def beside_kernel(
    count_ref,
    target_ref,
    source_ref,
    fill_ref,
    charges_hbm,
    basis_hbm,
    op_ref,
    mult_ref,
    local_ref,
    atoms_ref,
    number_ref,
    list_batch_ref,
    list_target_ref,
    list_source_ref,
    charges_ref,
    basis_ref,
    wide_ref,
    own_target,
    own_source,
    sems,
):
    cells = mult_ref.shape[0]
    batches = op_ref.shape[0]
    basis_copy = pltpu.make_async_copy(basis_hbm, basis_ref, sems.at[0])
    basis_copy.start()
    charges_copy = pltpu.make_async_copy(charges_hbm, charges_ref, sems.at[1])
    charges_copy.start()
    clear(local_ref, cells)
    basis_copy.wait()
    spread_basis(basis_ref, wide_ref)
    charges_copy.wait()

    def turn(i, carry):
        tile = masked_basis(wide_ref, count_ref, i, cells)
        mult_ref[i] = dot(tile.astype(BF), charges_ref[i]).astype(BF)
        atoms_ref[i] = jnp.pad(tile, ((0, 128 - ROWS), (0, 0))).T.astype(BF)
        return carry

    lax.fori_loop(0, cells, turn, 0, unroll=4)

    def batch(b, count):
        fill = fill_ref[b]
        base = 2 * count

        def sort(p, counts):
            own, far = counts
            source = source_ref[b, p]
            target = target_ref[b, p]
            is_own = source < cells

            @pl.when(is_own)
            def _():
                own_target[own] = target
                own_source[own] = source

            @pl.when(jnp.logical_not(is_own))
            def _():
                list_target_ref[base + far] = target
                list_source_ref[base + far] = source - cells

            step = is_own.astype(I32)
            return own + step, far + 1 - step

        own, far = lax.fori_loop(0, fill, sort, (0, 0))
        for q in range(8):
            own_target[own + q] = cells
            own_source[own + q] = 0
        list_target_ref[base + far] = cells
        list_source_ref[base + far] = 0
        doubles = (far + 1) // 2

        def mark(j, carry):
            list_batch_ref[count + j] = b
            return carry

        lax.fori_loop(0, doubles, mark, 0)
        op = op_ref[b][:, :ROWS]

        def chunk(j, carry):
            for q in range(0, 8, 2):
                p = j * 8 + q
                both = jnp.concatenate([mult_ref[own_source[p]], mult_ref[own_source[p + 1]]], axis=1)
                result = dot(op, both)
                local_ref[own_target[p]] += result[:, :128]
                local_ref[own_target[p + 1]] += result[:, 128:]
            return carry

        lax.fori_loop(0, (own + 7) // 8, chunk, 0)
        return count + doubles

    count = lax.fori_loop(0, batches, batch, 0)
    for q in range(UNROLL):
        list_batch_ref[count + q] = 0
        for side in range(2):
            list_target_ref[2 * (count + q) + side] = cells
            list_source_ref[2 * (count + q) + side] = 0
    number_ref[0] = (count + UNROLL - 1) // UNROLL


def pack_kernel(mult_hbm, back_hbm, out_hbm, asked_ref, mult_ref, back_ref, out_ref, wish_ref, sems, out_sems):
    remote = back_ref.shape[0]
    parts = 4
    step = remote // parts
    copies = []
    for part in range(parts):
        rows = pl.ds(part * step, step)
        copy = pltpu.make_async_copy(back_hbm.at[rows], back_ref.at[rows], sems.at[2 + part])
        copy.start()
        copies.append(copy)
    mult_copy = pltpu.make_async_copy(mult_hbm, mult_ref, sems.at[0])
    mult_copy.start()
    row = lax.broadcasted_iota(I32, (ROWS - MAIN, 128), 0)
    lane = lax.broadcasted_iota(I32, (ROWS - MAIN, 128), 1)

    def read(s, wish):
        tail = back_ref[s, MAIN:, :].astype(F32)
        return jnp.where((lane == s) & (row == 1), tail, wish)

    wish = jnp.zeros(row.shape, F32)
    for part in range(parts):
        copies[part].wait()
        wish = lax.fori_loop(part * step, (part + 1) * step, read, wish, unroll=16)
    wish_ref[...] = jnp.sum(wish, axis=0, keepdims=True).astype(I32)
    wish_copy = pltpu.make_async_copy(wish_ref, asked_ref, sems.at[1])
    wish_copy.start()
    mult_copy.wait()
    wish_copy.wait()

    def one(s, carry):
        out_ref[s] = mult_ref[asked_ref[0, s]]
        return carry

    outs = []
    for part in range(parts):
        lax.fori_loop(part * step, (part + 1) * step, one, 0, unroll=8)
        rows = pl.ds(part * step, step)
        copy = pltpu.make_async_copy(out_ref.at[rows], out_hbm.at[rows], out_sems.at[part])
        copy.start()
        outs.append(copy)
    for copy in outs:
        copy.wait()


def charge_kernel(asked_ref, returned_hbm, own_hbm, atoms_hbm, charge_hbm, returned_ref, own_ref, atoms_ref, charge_ref, sems):
    cells = own_ref.shape[0]
    remote = returned_ref.shape[0]
    copies = [
        pltpu.make_async_copy(src, dst, sems.at[k])
        for k, (src, dst) in enumerate(((own_hbm, own_ref), (returned_hbm, returned_ref), (atoms_hbm, atoms_ref)))
    ]
    for copy in copies:
        copy.start()
    for copy in copies:
        copy.wait()

    def collect(s, carry):
        own_ref[asked_ref[0, s]] += returned_ref[s].astype(F32)
        return carry

    lax.fori_loop(0, remote, collect, 0, unroll=4)

    row = lax.broadcasted_iota(I32, (ROWS, 128), 0)

    def atoms(i, carry):
        grads = jnp.where(row > MAIN, 0.0, own_ref[i]).astype(BF)
        charge_ref[i] = dot(atoms_ref[i][:, :ROWS], grads).astype(BF)
        return carry

    lax.fori_loop(0, cells, atoms, 0, unroll=4)
    out = pltpu.make_async_copy(charge_ref, charge_hbm, sems.at[0])
    out.start()
    out.wait()


def far_kernel(
    number_ref,
    list_batch_ref,
    list_target_ref,
    list_source_ref,
    incoming_hbm,
    local_hbm,
    atoms_hbm,
    op_hbm,
    potential_hbm,
    incoming_ref,
    local_ref,
    atoms_ref,
    op_ref,
    potential_ref,
    sems,
    out_sems,
):
    cells = atoms_ref.shape[0]
    copies = [
        pltpu.make_async_copy(src, dst, sems.at[k])
        for k, (src, dst) in enumerate(
            ((op_hbm, op_ref), (incoming_hbm, incoming_ref), (local_hbm, local_ref), (atoms_hbm, atoms_ref))
        )
    ]
    for copy in copies:
        copy.start()
    for copy in copies[:3]:
        copy.wait()

    def turn(j, carry):
        for q in range(UNROLL):
            d = j * UNROLL + q
            both = jnp.concatenate(
                [incoming_ref[list_source_ref[2 * d]], incoming_ref[list_source_ref[2 * d + 1]]], axis=1
            )
            result = dot(op_ref[list_batch_ref[d]][:, :ROWS], both)
            local_ref[list_target_ref[2 * d]] += result[:, :128]
            local_ref[list_target_ref[2 * d + 1]] += result[:, 128:]
        return carry

    lax.fori_loop(0, number_ref[0], turn, 0)
    copies[3].wait()

    def atoms(i, carry):
        potential_ref[i] = dot(atoms_ref[i][:, :ROWS], local_ref[i].astype(BF)).astype(BF)
        return carry

    outs = []
    parts = 4
    width = cells // parts
    for part in range(parts):
        lax.fori_loop(part * width, (part + 1) * width, atoms, 0, unroll=8)
        rows = pl.ds(part * width, width)
        copy = pltpu.make_async_copy(potential_ref.at[rows], potential_hbm.at[rows], out_sems.at[part])
        copy.start()
        outs.append(copy)
    for copy in outs:
        copy.wait()


SMEM = pl.BlockSpec(memory_space=pltpu.SMEM)
VMEM = pl.BlockSpec(memory_space=pltpu.VMEM)
ANY = pl.BlockSpec(memory_space=pl.ANY)
Shape = jax.ShapeDtypeStruct


def call_back(leaf_count, targets, sources, fill, wishes, cotangent, basis_major, chosen):
    coeffs, cells, slots = basis_major.shape
    domains = wishes.shape[1]
    batches, batch_size = targets.shape
    channels = cotangent.shape[2]
    return pl.pallas_call(
        back_kernel,
        out_shape=(
            Shape((domains, ROWS, channels), BF),
            Shape((cells, ROWS, channels), F32),
            Shape((batches, ROWS, 128), BF),
        ),
        in_specs=[SMEM] * 5 + [ANY] * 2 + [VMEM],
        out_specs=(ANY, ANY, VMEM),
        scratch_shapes=[
            pltpu.VMEM((cells, slots, channels), BF),
            pltpu.VMEM((coeffs, cells, slots), BF),
            pltpu.VMEM((ROWS * cells, slots), F32),
            pltpu.VMEM((cells, ROWS, channels), BF),
            pltpu.VMEM((cells + domains + 1, ROWS, channels), F32),
            pltpu.VMEM((domains, ROWS, channels), BF),
            pltpu.VMEM((batches, ROWS, 128), BF),
            pltpu.SMEM((batches * batch_size // 2 + UNROLL,), I32),
            pltpu.SemaphoreType.DMA((5,)),
            pltpu.SemaphoreType.DMA((4,)),
        ],
        compiler_params=params(LIMIT),
        name="back_pairs",
    )(leaf_count, targets, sources, fill, wishes, cotangent, basis_major, chosen)


def call_beside(leaf_count, targets, sources, fill, charges, basis_major, ops):
    coeffs, cells, slots = basis_major.shape
    batches, batch_size = targets.shape
    channels = charges.shape[2]
    doubles = batches * (batch_size // 2) + UNROLL
    return pl.pallas_call(
        beside_kernel,
        out_shape=(
            Shape((cells, ROWS, channels), BF),
            Shape((cells + 1, ROWS, channels), F32),
            Shape((cells, slots, 128), BF),
            Shape((1,), I32),
            Shape((doubles,), I32),
            Shape((2 * doubles,), I32),
            Shape((2 * doubles,), I32),
        ),
        in_specs=[SMEM] * 4 + [ANY] * 2 + [VMEM],
        out_specs=(VMEM, VMEM, VMEM, SMEM, SMEM, SMEM, SMEM),
        scratch_shapes=[
            pltpu.VMEM((cells, slots, channels), BF),
            pltpu.VMEM((coeffs, cells, slots), BF),
            pltpu.VMEM((ROWS * cells, slots), F32),
            pltpu.SMEM((batch_size + 8,), I32),
            pltpu.SMEM((batch_size + 8,), I32),
            pltpu.SemaphoreType.DMA((2,)),
        ],
        compiler_params=params(LIMIT),
        cost_estimate=pl.CostEstimate(flops=400_000_000, bytes_accessed=8_000_000, transcendentals=0),
        name="own_pairs",
    )(leaf_count, targets, sources, fill, charges, basis_major, ops)


def call_pack(mult, returned):
    cells, _, channels = mult.shape
    domains = returned.shape[0]
    return pl.pallas_call(
        pack_kernel,
        out_shape=(Shape((domains, ROWS, channels), BF), Shape((1, domains), I32)),
        in_specs=[ANY] * 2,
        out_specs=(ANY, SMEM),
        scratch_shapes=[
            pltpu.VMEM((cells, ROWS, channels), BF),
            pltpu.VMEM((domains, ROWS, channels), BF),
            pltpu.VMEM((domains, ROWS, channels), BF),
            pltpu.VMEM((1, domains), I32),
            pltpu.SemaphoreType.DMA((6,)),
            pltpu.SemaphoreType.DMA((4,)),
        ],
        compiler_params=params(LIMIT),
        name="pack_blocks",
    )(mult, returned)


def call_charge(asked, returned, own, atoms):
    cells, slots, _ = atoms.shape
    domains, _, channels = returned.shape
    return pl.pallas_call(
        charge_kernel,
        out_shape=Shape((cells, slots, channels), BF),
        in_specs=[SMEM] + [ANY] * 3,
        out_specs=ANY,
        scratch_shapes=[
            pltpu.VMEM((domains, ROWS, channels), BF),
            pltpu.VMEM((cells, ROWS, channels), F32),
            pltpu.VMEM((cells, slots, 128), BF),
            pltpu.VMEM((cells, slots, channels), BF),
            pltpu.SemaphoreType.DMA((3,)),
        ],
        compiler_params=params(LIMIT),
        cost_estimate=pl.CostEstimate(flops=200_000_000, bytes_accessed=8_000_000, transcendentals=0),
        name="charge_atoms",
    )(asked, returned, own, atoms)


def call_far(number, list_batch, list_target, list_source, incoming, local_part, atoms, ops):
    cells, slots, _ = atoms.shape
    domains, _, channels = incoming.shape
    return pl.pallas_call(
        far_kernel,
        out_shape=Shape((cells, slots, channels), BF),
        in_specs=[SMEM] * 4 + [ANY] * 4,
        out_specs=ANY,
        scratch_shapes=[
            pltpu.VMEM((domains, ROWS, channels), BF),
            pltpu.VMEM((cells + 1, ROWS, channels), F32),
            pltpu.VMEM((cells, slots, 128), BF),
            pltpu.VMEM(ops.shape, BF),
            pltpu.VMEM((cells, slots, channels), BF),
            pltpu.SemaphoreType.DMA((4,)),
            pltpu.SemaphoreType.DMA((4,)),
        ],
        compiler_params=params(LIMIT),
        name="far_pairs_atoms",
    )(number, list_batch, list_target, list_source, incoming, local_part, atoms, ops)


def choose(batch_class, m2l_ops):
    hot = (batch_class[:, None] == lax.broadcasted_iota(I32, (1, m2l_ops.shape[0]), 1)).astype(BF)
    return jnp.einsum("bn,nkl->bkl", hot, m2l_ops, preferred_element_type=F32).astype(BF)


def local(
    charges,
    basis,
    leaf_count,
    cotangent,
    m2l_ops,
    fetch_cells,
    pair_target,
    pair_source,
    batch_class,
    batch_fill,
):
    basis_major = basis.transpose(1, 0, 2)
    wishes = fetch_cells.reshape(1, -1)
    targets, sources, fill = pair_target[0], pair_source[0], batch_fill[0]
    chosen = choose(batch_class[0], m2l_ops)
    back, own, ops = call_back(leaf_count, targets, sources, fill, wishes, cotangent, basis_major, chosen)
    returned = lax.all_to_all(back, ("dx", "dy"), split_axis=0, concat_axis=0, tiled=True)
    mult, local_part, atoms, number, list_batch, list_target, list_source = call_beside(
        leaf_count, targets, sources, fill, charges, basis_major, ops
    )
    outgoing, asked = call_pack(mult, returned)
    incoming = lax.all_to_all(outgoing, ("dx", "dy"), split_axis=0, concat_axis=0, tiled=True)
    charge_grad = call_charge(asked, returned, own, atoms)
    potential = call_far(number, list_batch, list_target, list_source, incoming, local_part, atoms, ops)
    return potential, charge_grad


def solution(mesh):
    in_specs = (
        P(("dx", "dy"), None, None),
        P(("dx", "dy"), None, None),
        P(("dx", "dy")),
        P(("dx", "dy"), None, None),
        P(),
        P(("dx", "dy"), None, None),
        P(("dx", "dy"), None, None),
        P(("dx", "dy"), None, None),
        P(("dx", "dy"), None),
        P(("dx", "dy"), None),
    )
    out_specs = (P(("dx", "dy"), None, None), P(("dx", "dy"), None, None))
    return jax.shard_map(local, mesh=mesh, in_specs=in_specs, out_specs=out_specs, check_vma=False)
```

```python
import jax
import jax.numpy as jnp
from jax import lax
from jax.experimental import pallas as pl
from jax.experimental.pallas import tpu as pltpu
from jax.sharding import PartitionSpec as P

BF = jnp.bfloat16
F32 = jnp.float32
I32 = jnp.int32
ROWS = 88
MAIN = 80
KEEP = 82
STRIDE = 72
UNROLL = 16
LIMIT = 62


def dot(a, b):
    return lax.dot_general(a, b, (((1,), (0,)), ((), ())), preferred_element_type=F32)


def params():
    return pltpu.CompilerParams(vmem_limit_bytes=LIMIT << 20)


def flat(ref):
    return ref.reshape(ref.shape[0] * KEEP, ref.shape[-1])


def block(index):
    return pl.ds(pl.multiple_of(index * KEEP, 2), KEEP)


def spread_basis(basis_ref, wide_ref):
    coeffs, cells, slots = basis_ref.shape

    def put(k, carry):
        wide_ref[pl.ds(pl.multiple_of(k * STRIDE, 8), cells), :] = basis_ref[k].astype(F32)
        return carry

    lax.fori_loop(0, coeffs, put, 0, unroll=9)
    wide_ref[coeffs * STRIDE :, :] = jnp.zeros(((ROWS - coeffs) * STRIDE, slots), F32)


def masked_basis(wide_ref, count_ref, cell):
    tile = wide_ref[pl.ds(cell, ROWS, stride=STRIDE), :]
    lane = lax.broadcasted_iota(I32, tile.shape, 1)
    return jnp.where(lane < count_ref[cell], tile, 0.0)


def clear(ref, count):
    def one(e, carry):
        ref[e] = jnp.zeros(ref.shape[1:], ref.dtype)
        return carry

    lax.fori_loop(0, count, one, 0, unroll=8)


def encode(batch, entry, target):
    return batch * 65536 + entry * 256 + target


def decode(code):
    return code >> 16, (code >> 8) & 255, code & 255


def back_kernel(
    count_ref,
    target_ref,
    source_ref,
    fill_ref,
    fetch_ref,
    cotangent_hbm,
    basis_hbm,
    chosen_hbm,
    back_hbm,
    cotangent_ref,
    basis_ref,
    chosen_ref,
    wide_ref,
    grad_ref,
    total_ref,
    back_ref,
    back_op_ref,
    list_ref,
    sems,
    out_sems,
):
    cells = cotangent_ref.shape[0]
    coeffs = basis_ref.shape[0]
    batches, batch_size = target_ref.shape
    remote = back_ref.shape[0]
    parts = 4
    step = cells // parts
    basis_copy = pltpu.make_async_copy(basis_hbm, basis_ref, sems.at[0])
    basis_copy.start()
    copies = []
    for part in range(parts):
        rows = pl.ds(part * step, step)
        copy = pltpu.make_async_copy(cotangent_hbm.at[rows], cotangent_ref.at[rows], sems.at[2 + part])
        copy.start()
        copies.append(copy)
    chosen_copy = pltpu.make_async_copy(chosen_hbm, chosen_ref, sems.at[1])
    chosen_copy.start()
    clear(total_ref, remote)
    basis_copy.wait()
    spread_basis(basis_ref, wide_ref)

    share = cells // batches
    slots = batch_size // share
    dummy = encode(0, remote, 0)

    def moments(b, place):
        fill = fill_ref[b]
        for q in range(share):
            i = b * share + q
            tile = masked_basis(wide_ref, count_ref, i).astype(BF)
            grad_ref[i] = dot(tile, cotangent_ref[i]).astype(BF)
            for p in range(q * slots, (q + 1) * slots):
                entry = source_ref[b, p] - cells
                list_ref[place] = encode(b, entry, target_ref[b, p])
                place += jnp.where((p < fill) & (entry >= 0), 1, 0)
        list_ref[place] = dummy
        return ((place + 1) // 2) * 2

    place = 0
    for part in range(parts):
        copies[part].wait()
        place = lax.fori_loop(part * batches // parts, (part + 1) * batches // parts, moments, place)
    for q in range(2 * UNROLL):
        list_ref[place + q] = dummy
    turns = (place + 2 * UNROLL - 1) // (2 * UNROLL)
    chosen_copy.wait()

    def prepare(b, carry):
        wide = jnp.pad(chosen_ref[b].astype(F32), ((0, 128 - coeffs), (0, 128 - coeffs)))
        back_op_ref[b] = wide.T[:ROWS].astype(BF)
        return carry

    lax.fori_loop(0, batches, prepare, 0, unroll=4)

    def turn(j, carry):
        for q in range(UNROLL):
            d = 2 * (j * UNROLL + q)
            b, e0, t0 = decode(list_ref[d])
            _, e1, t1 = decode(list_ref[d + 1])
            result = dot(back_op_ref[b][:, :ROWS], jnp.concatenate([grad_ref[t0], grad_ref[t1]], axis=1))
            total_ref[e0] += result[:, :128]
            total_ref[e1] += result[:, 128:]
        return carry

    lax.fori_loop(0, turns, turn, 0)
    row = lax.broadcasted_iota(I32, (ROWS - MAIN, 128), 0)
    packed = flat(back_ref)

    def narrow(s, carry):
        tail = jnp.where(row == 1, fetch_ref[0, s].astype(F32), total_ref[s, MAIN:, :])
        tile = jnp.concatenate([total_ref[s, :MAIN, :], tail], axis=0).astype(BF)
        packed[block(s), :] = tile[:KEEP]
        return carry

    outs = []
    width = remote // parts
    for part in range(parts):
        lax.fori_loop(part * width, (part + 1) * width, narrow, 0, unroll=8)
        rows = pl.ds(part * width, width)
        copy = pltpu.make_async_copy(back_ref.at[rows], back_hbm.at[rows], out_sems.at[part])
        copy.start()
        outs.append(copy)
    for copy in outs:
        copy.wait()


def beside_kernel(
    count_ref,
    target_ref,
    source_ref,
    fill_ref,
    charges_hbm,
    cotangent_hbm,
    basis_hbm,
    chosen_ref,
    mult_hbm,
    local_ref,
    own_ref,
    atoms_ref,
    op_ref,
    list_ref,
    charges_ref,
    cotangent_ref,
    basis_ref,
    wide_ref,
    mult_ref,
    packed_ref,
    grad_ref,
    back_op_ref,
    own_target,
    own_source,
    sems,
):
    cells = mult_ref.shape[0]
    coeffs = basis_ref.shape[0]
    batches, _, _ = chosen_ref.shape
    copies = [
        pltpu.make_async_copy(src, dst, sems.at[k])
        for k, (src, dst) in enumerate(
            ((basis_hbm, basis_ref), (charges_hbm, charges_ref), (cotangent_hbm, cotangent_ref))
        )
    ]
    for copy in copies:
        copy.start()
    clear(local_ref, cells)
    clear(own_ref, cells)
    for copy in copies:
        copy.wait()
    spread_basis(basis_ref, wide_ref)
    packed = flat(packed_ref)

    def turn(i, carry):
        tile = masked_basis(wide_ref, count_ref, i)
        both = jnp.concatenate([charges_ref[i], cotangent_ref[i]], axis=1)
        result = dot(tile.astype(BF), both).astype(BF)
        mult_ref[i] = result[:, :128]
        packed[block(i), :] = result[:KEEP, :128]
        grad_ref[i] = result[:, 128:]
        atoms_ref[i] = jnp.pad(tile, ((0, 128 - ROWS), (0, 0))).T.astype(BF)
        return carry

    lax.fori_loop(0, cells, turn, 0, unroll=4)
    mult_copy = pltpu.make_async_copy(packed_ref, mult_hbm, sems.at[0])
    mult_copy.start()

    def prepare(b, carry):
        wide = jnp.pad(chosen_ref[b].astype(F32), ((0, 128 - coeffs), (0, 128 - coeffs)))
        back_op_ref[b] = wide.T[:ROWS].astype(BF)
        op_ref[b] = wide[:ROWS].astype(BF)
        return carry

    lax.fori_loop(0, batches, prepare, 0, unroll=2)
    dummy = encode(0, 0, cells)

    def batch(b, place):
        fill = fill_ref[b]

        def sort(p, places):
            own, far = places
            entry = source_ref[b, p] - cells
            target = target_ref[b, p]
            is_far = entry >= 0

            @pl.when(is_far)
            def _():
                list_ref[far] = encode(b, entry, target)

            @pl.when(jnp.logical_not(is_far))
            def _():
                own_target[own] = target
                own_source[own] = entry + cells

            step = is_far.astype(I32)
            return own + 1 - step, far + step

        own, far = lax.fori_loop(0, fill, sort, (0, place))
        list_ref[far] = dummy
        for q in range(8):
            own_target[own + q] = cells
            own_source[own + q] = cells
        op = op_ref[b][:, :ROWS]
        back_op = back_op_ref[b][:, :ROWS]

        def chunk(j, carry):
            for q in range(0, 8, 2):
                t0, t1 = own_target[j * 8 + q], own_target[j * 8 + q + 1]
                e0, e1 = own_source[j * 8 + q], own_source[j * 8 + q + 1]
                result = dot(op, jnp.concatenate([mult_ref[jnp.minimum(e0, cells - 1)], mult_ref[jnp.minimum(e1, cells - 1)]], axis=1))
                local_ref[t0] += result[:, :128]
                local_ref[t1] += result[:, 128:]
                result = dot(back_op, jnp.concatenate([grad_ref[jnp.minimum(t0, cells - 1)], grad_ref[jnp.minimum(t1, cells - 1)]], axis=1))
                own_ref[e0] += result[:, :128]
                own_ref[e1] += result[:, 128:]
            return carry

        lax.fori_loop(0, (own + 7) // 8, chunk, 0)
        return ((far + 1) // 2) * 2

    place = lax.fori_loop(0, batches, batch, 2)
    for q in range(2 * UNROLL):
        list_ref[place + q] = dummy
    list_ref[0] = (place - 2 + 2 * UNROLL - 1) // (2 * UNROLL)
    list_ref[1] = 0
    mult_copy.wait()


def pack_kernel(mult_hbm, back_hbm, out_hbm, asked_ref, mult_ref, tail_ref, wish_ref, sems):
    remote = back_hbm.shape[0]
    tail_copy = pltpu.make_async_copy(back_hbm.at[:, pl.ds(MAIN // 2, 1)], tail_ref, sems.at[0])
    tail_copy.start()
    mult_copy = pltpu.make_async_copy(mult_hbm, mult_ref, sems.at[1])
    mult_copy.start()
    row = lax.broadcasted_iota(I32, (16, 128), 0)
    lane = lax.broadcasted_iota(I32, (16, 128), 1)
    tails = tail_ref.reshape(2 * remote, 128)
    tail_copy.wait()
    wish = jnp.zeros((16, 128), F32)
    for g in range(remote // 8):
        tile = tails[16 * g : 16 * g + 16, :].astype(F32)
        wish = jnp.where(row == 2 * (lane - 8 * g) + 1, tile, wish)
    wish_ref[...] = jnp.sum(wish, axis=0, keepdims=True).astype(I32)
    wish_copy = pltpu.make_async_copy(wish_ref, asked_ref, sems.at[2])
    wish_copy.start()
    mult_copy.wait()
    wish_copy.wait()

    def one(s, carry):
        pltpu.make_async_copy(mult_ref.at[asked_ref[0, s]], out_hbm.at[s], sems.at[3]).start()
        return carry

    lax.fori_loop(0, remote, one, 0, unroll=8)
    pltpu.make_async_copy(back_hbm, out_hbm, sems.at[3]).wait()


def charge_kernel(asked_ref, returned_hbm, own_hbm, atoms_hbm, charge_hbm, returned_ref, own_ref, atoms_ref, charge_ref, sems):
    cells = charge_ref.shape[0]
    remote = returned_ref.shape[0]
    copies = [
        pltpu.make_async_copy(src, dst, sems.at[k])
        for k, (src, dst) in enumerate(((own_hbm, own_ref), (returned_hbm, returned_ref), (atoms_hbm, atoms_ref)))
    ]
    for copy in copies:
        copy.start()
    for copy in copies:
        copy.wait()
    packed = flat(returned_ref)

    def collect(s, carry):
        own_ref[asked_ref[0, s], :KEEP, :] += packed[block(s), :].astype(F32)
        return carry

    lax.fori_loop(0, remote, collect, 0, unroll=4)
    row = lax.broadcasted_iota(I32, (ROWS, 128), 0)

    def atoms(i, carry):
        grads = jnp.where(row > MAIN, 0.0, own_ref[i]).astype(BF)
        charge_ref[i] = dot(atoms_ref[i][:, :ROWS], grads).astype(BF)
        return carry

    lax.fori_loop(0, cells, atoms, 0, unroll=4)
    out = pltpu.make_async_copy(charge_ref, charge_hbm, sems.at[0])
    out.start()
    out.wait()


def far_kernel(
    list_ref,
    incoming_hbm,
    local_hbm,
    atoms_hbm,
    op_hbm,
    potential_hbm,
    incoming_ref,
    local_ref,
    atoms_ref,
    op_ref,
    sum_ref,
    potential_ref,
    sems,
    out_sems,
):
    cells = atoms_ref.shape[0]
    copies = [
        pltpu.make_async_copy(src, dst, sems.at[k])
        for k, (src, dst) in enumerate(
            ((op_hbm, op_ref), (incoming_hbm, incoming_ref), (local_hbm, local_ref), (atoms_hbm, atoms_ref))
        )
    ]
    for copy in copies:
        copy.start()
    clear(sum_ref, cells)
    packed = flat(incoming_ref)
    for copy in copies[:2]:
        copy.wait()

    def turn(j, carry):
        for q in range(UNROLL):
            d = 2 * (j * UNROLL + q + 1)
            b, e0, t0 = decode(list_ref[d])
            _, e1, t1 = decode(list_ref[d + 1])
            both = jnp.concatenate([packed[block(e0), :], packed[block(e1), :]], axis=1)
            result = dot(op_ref[b][:, :KEEP], both)
            sum_ref[t0] += result[:, :128]
            sum_ref[t1] += result[:, 128:]
        return carry

    lax.fori_loop(0, list_ref[0], turn, 0)
    for copy in copies[2:]:
        copy.wait()

    def atoms(i, carry):
        whole = (sum_ref[i] + local_ref[i]).astype(BF)
        potential_ref[i] = dot(atoms_ref[i][:, :ROWS], whole).astype(BF)
        return carry

    outs = []
    parts = 4
    width = cells // parts
    for part in range(parts):
        lax.fori_loop(part * width, (part + 1) * width, atoms, 0, unroll=8)
        rows = pl.ds(part * width, width)
        copy = pltpu.make_async_copy(potential_ref.at[rows], potential_hbm.at[rows], out_sems.at[part])
        copy.start()
        outs.append(copy)
    for copy in outs:
        copy.wait()


SMEM = pl.BlockSpec(memory_space=pltpu.SMEM)
VMEM = pl.BlockSpec(memory_space=pltpu.VMEM)
ANY = pl.BlockSpec(memory_space=pl.ANY)
Shape = jax.ShapeDtypeStruct


def call_back(leaf_count, targets, sources, fill, wishes, cotangent, basis_major, chosen):
    coeffs, cells, slots = basis_major.shape
    domains = wishes.shape[1]
    batches, batch_size = targets.shape
    channels = cotangent.shape[2]
    return pl.pallas_call(
        back_kernel,
        out_shape=Shape((domains, KEEP // 2, 2, channels), BF),
        in_specs=[SMEM] * 5 + [ANY] * 3,
        out_specs=ANY,
        scratch_shapes=[
            pltpu.VMEM((cells, slots, channels), BF),
            pltpu.VMEM((coeffs, cells, slots), BF),
            pltpu.VMEM(chosen.shape, BF),
            pltpu.VMEM((ROWS * STRIDE, slots), F32),
            pltpu.VMEM((cells, ROWS, channels), BF),
            pltpu.VMEM((domains + 1, ROWS, channels), F32),
            pltpu.VMEM((domains, KEEP // 2, 2, channels), BF),
            pltpu.VMEM((batches, ROWS, 128), BF),
            pltpu.SMEM((batches * batch_size + 2 * UNROLL + 2,), I32),
            pltpu.SemaphoreType.DMA((6,)),
            pltpu.SemaphoreType.DMA((4,)),
        ],
        compiler_params=params(),
        name="back_pairs",
    )(leaf_count, targets, sources, fill, wishes, cotangent, basis_major, chosen)


def call_beside(leaf_count, targets, sources, fill, charges, cotangent, basis_major, chosen):
    coeffs, cells, slots = basis_major.shape
    batches, batch_size = targets.shape
    channels = charges.shape[2]
    return pl.pallas_call(
        beside_kernel,
        out_shape=(
            Shape((cells, KEEP // 2, 2, channels), BF),
            Shape((cells + 1, ROWS, channels), F32),
            Shape((cells + 1, ROWS, channels), F32),
            Shape((cells, slots, 128), BF),
            Shape((batches, ROWS, 128), BF),
            Shape((batches * batch_size + 2 * UNROLL + 4,), I32),
        ),
        in_specs=[SMEM] * 4 + [ANY] * 3 + [VMEM],
        out_specs=(ANY, VMEM, VMEM, VMEM, VMEM, SMEM),
        scratch_shapes=[
            pltpu.VMEM((cells, slots, channels), BF),
            pltpu.VMEM((cells, slots, channels), BF),
            pltpu.VMEM((coeffs, cells, slots), BF),
            pltpu.VMEM((ROWS * STRIDE, slots), F32),
            pltpu.VMEM((cells, ROWS, channels), BF),
            pltpu.VMEM((cells, KEEP // 2, 2, channels), BF),
            pltpu.VMEM((cells, ROWS, channels), BF),
            pltpu.VMEM((batches, ROWS, 128), BF),
            pltpu.SMEM((batch_size + 8,), I32),
            pltpu.SMEM((batch_size + 8,), I32),
            pltpu.SemaphoreType.DMA((3,)),
        ],
        compiler_params=params(),
        cost_estimate=pl.CostEstimate(flops=400_000_000, bytes_accessed=8_000_000, transcendentals=0),
        name="own_pairs",
    )(leaf_count, targets, sources, fill, charges, cotangent, basis_major, chosen)


def call_pack(mult, returned):
    cells, _, _, channels = mult.shape
    domains = returned.shape[0]
    return pl.pallas_call(
        pack_kernel,
        out_shape=(Shape(returned.shape, BF), Shape((1, domains), I32)),
        in_specs=[ANY] * 2,
        out_specs=(ANY, SMEM),
        scratch_shapes=[
            pltpu.VMEM(mult.shape, BF),
            pltpu.VMEM((domains, 1, 2, channels), BF),
            pltpu.VMEM((1, domains), I32),
            pltpu.SemaphoreType.DMA((4,)),
        ],
        compiler_params=params(),
        name="pack_blocks",
    )(mult, returned)


def call_charge(asked, returned, own, atoms):
    cells, slots, _ = atoms.shape
    channels = returned.shape[3]
    return pl.pallas_call(
        charge_kernel,
        out_shape=Shape((cells, slots, channels), BF),
        in_specs=[SMEM] + [ANY] * 3,
        out_specs=ANY,
        scratch_shapes=[
            pltpu.VMEM(returned.shape, BF),
            pltpu.VMEM(own.shape, F32),
            pltpu.VMEM((cells, slots, 128), BF),
            pltpu.VMEM((cells, slots, channels), BF),
            pltpu.SemaphoreType.DMA((3,)),
        ],
        compiler_params=params(),
        cost_estimate=pl.CostEstimate(flops=200_000_000, bytes_accessed=8_000_000, transcendentals=0),
        name="charge_atoms",
    )(asked, returned, own, atoms)


def call_far(pairs, incoming, local_part, atoms, ops):
    cells, slots, _ = atoms.shape
    channels = incoming.shape[3]
    return pl.pallas_call(
        far_kernel,
        out_shape=Shape((cells, slots, channels), BF),
        in_specs=[SMEM] + [ANY] * 4,
        out_specs=ANY,
        scratch_shapes=[
            pltpu.VMEM(incoming.shape, BF),
            pltpu.VMEM(local_part.shape, F32),
            pltpu.VMEM((cells, slots, 128), BF),
            pltpu.VMEM(ops.shape, BF),
            pltpu.VMEM((cells + 1, ROWS, channels), F32),
            pltpu.VMEM((cells, slots, channels), BF),
            pltpu.SemaphoreType.DMA((4,)),
            pltpu.SemaphoreType.DMA((4,)),
        ],
        compiler_params=params(),
        name="far_pairs_atoms",
    )(pairs, incoming, local_part, atoms, ops)


def choose(batch_class, m2l_ops):
    hot = (batch_class[:, None] == lax.broadcasted_iota(I32, (1, m2l_ops.shape[0]), 1)).astype(BF)
    return jnp.einsum("bn,nkl->bkl", hot, m2l_ops, preferred_element_type=F32).astype(BF)


def local(
    charges,
    basis,
    leaf_count,
    cotangent,
    m2l_ops,
    fetch_cells,
    pair_target,
    pair_source,
    batch_class,
    batch_fill,
):
    basis_major = basis.transpose(1, 0, 2)
    wishes = fetch_cells.reshape(1, -1)
    targets, sources, fill = pair_target[0], pair_source[0], batch_fill[0]
    chosen = choose(batch_class[0], m2l_ops)
    back = call_back(leaf_count, targets, sources, fill, wishes, cotangent, basis_major, chosen)
    returned = lax.all_to_all(back, ("dx", "dy"), split_axis=0, concat_axis=0, tiled=True)
    mult, local_part, own, atoms, ops, pairs = call_beside(
        leaf_count, targets, sources, fill, charges, cotangent, basis_major, chosen
    )
    outgoing, asked = call_pack(mult, returned)
    incoming = lax.all_to_all(outgoing, ("dx", "dy"), split_axis=0, concat_axis=0, tiled=True)
    charge_grad = call_charge(asked, returned, own, atoms)
    potential = call_far(pairs, incoming, local_part, atoms, ops)
    return potential, charge_grad


def solution(mesh):
    in_specs = (
        P(("dx", "dy"), None, None),
        P(("dx", "dy"), None, None),
        P(("dx", "dy")),
        P(("dx", "dy"), None, None),
        P(),
        P(("dx", "dy"), None, None),
        P(("dx", "dy"), None, None),
        P(("dx", "dy"), None, None),
        P(("dx", "dy"), None),
        P(("dx", "dy"), None),
    )
    out_specs = (P(("dx", "dy"), None, None), P(("dx", "dy"), None, None))
    return jax.shard_map(local, mesh=mesh, in_specs=in_specs, out_specs=out_specs, check_vma=False)
```

```python
import jax
import jax.numpy as jnp
from jax import lax
from jax.experimental import pallas as pl
from jax.experimental.pallas import tpu as pltpu
from jax.sharding import PartitionSpec as P

BF = jnp.bfloat16
F32 = jnp.float32
I32 = jnp.int32
ROWS = 88
MAIN = 80
KEEP = 82
STRIDE = 72
UNROLL = 16
LIMIT = 62


def dot(a, b):
    return lax.dot_general(a, b, (((1,), (0,)), ((), ())), preferred_element_type=F32)


def params():
    return pltpu.CompilerParams(vmem_limit_bytes=LIMIT << 20)


def flat(ref):
    return ref.reshape(ref.shape[0] * KEEP, ref.shape[-1])


def block(index):
    return pl.ds(pl.multiple_of(index * KEEP, 2), KEEP)


def spread_basis(basis_ref, wide_ref):
    coeffs, cells, slots = basis_ref.shape

    def put(k, carry):
        wide_ref[pl.ds(pl.multiple_of(k * STRIDE, 8), cells), :] = basis_ref[k].astype(F32)
        return carry

    lax.fori_loop(0, coeffs, put, 0, unroll=9)
    wide_ref[coeffs * STRIDE :, :] = jnp.zeros(((ROWS - coeffs) * STRIDE, slots), F32)


def masked_basis(wide_ref, count_ref, cell):
    tile = wide_ref[pl.ds(cell, ROWS, stride=STRIDE), :]
    lane = lax.broadcasted_iota(I32, tile.shape, 1)
    return jnp.where(lane < count_ref[cell], tile, 0.0)


def clear(ref, count):
    def one(e, carry):
        ref[e] = jnp.zeros(ref.shape[1:], ref.dtype)
        return carry

    lax.fori_loop(0, count, one, 0, unroll=8)


def encode(batch, entry, target):
    return batch * 65536 + entry * 256 + target


def decode(code):
    return code >> 16, (code >> 8) & 255, code & 255


def choose_operators(class_ref, ops_ref, rows_ref):
    coeffs, _, classes = ops_ref.shape
    batches = rows_ref.shape[0] // ROWS
    rows_ref[...] = jnp.zeros(rows_ref.shape, F32)
    row = lax.broadcasted_iota(I32, (batches, classes), 0)
    wanted = jnp.zeros((batches, classes), I32)
    for b in range(batches):
        wanted = jnp.where(row == b, class_ref[b], wanted)
    hot = (wanted == lax.broadcasted_iota(I32, (batches, classes), 1)).astype(F32).astype(BF)

    def one(k, carry):
        picked = lax.dot_general(hot, ops_ref[k], (((1,), (1,)), ((), ())), preferred_element_type=F32)
        rows_ref[pl.ds(pl.multiple_of(k * batches, batches), batches), :coeffs] = picked
        return carry

    return one


def back_kernel(
    count_ref,
    fill_ref,
    fetch_ref,
    class_ref,
    target_ref,
    source_ref,
    cotangent_hbm,
    basis_hbm,
    ops_hbm,
    back_hbm,
    op_hbm,
    cotangent_ref,
    basis_ref,
    ops_ref,
    wide_ref,
    rows_ref,
    grad_ref,
    total_ref,
    back_ref,
    op_ref,
    back_op_ref,
    found_ref,
    code_ref,
    list_ref,
    sems,
    ops_sems,
    out_sems,
):
    cells = cotangent_ref.shape[0]
    coeffs = basis_ref.shape[0]
    batches, batch_size = target_ref.shape
    remote = back_ref.shape[0]
    parts = 4
    step = cells // parts
    span = coeffs // parts
    basis_copy = pltpu.make_async_copy(basis_hbm, basis_ref, sems.at[parts])
    basis_copy.start()

    def cotangent_copy(part):
        rows = pl.ds(part * step, step)
        return pltpu.make_async_copy(cotangent_hbm.at[rows], cotangent_ref.at[rows], sems.at[part])

    def ops_copy(part):
        rows = pl.ds(part * span, span)
        return pltpu.make_async_copy(ops_hbm.at[rows], ops_ref.at[rows], ops_sems.at[part])

    for part in range(parts):
        cotangent_copy(part).start()
        ops_copy(part).start()
    rows = pl.ds(parts * span, coeffs - parts * span)
    rest_copy = pltpu.make_async_copy(ops_hbm.at[rows], ops_ref.at[rows], ops_sems.at[parts])
    rest_copy.start()

    batch = lax.broadcasted_iota(I32, (batches, batch_size), 0)
    slot = lax.broadcasted_iota(I32, (batches, batch_size), 1)
    fill = jnp.zeros((batches, batch_size), I32)
    for b in range(batches):
        fill = jnp.where(batch == b, fill_ref[b], fill)
    entry = source_ref[...] - cells
    far = (slot < fill) & (entry >= 0)
    found_ref[...] = jnp.where(far, encode(batch, entry, target_ref[...]), -1)
    code_copy = pltpu.make_async_copy(found_ref, code_ref, sems.at[parts + 1])
    code_copy.start()
    clear(total_ref, remote)
    choose = choose_operators(class_ref, ops_ref, rows_ref)
    basis_copy.wait()
    spread_basis(basis_ref, wide_ref)
    code_copy.wait()

    share = cells // batches
    slots = batch_size // share
    dummy = encode(0, remote, 0)
    group = batches // parts

    def moments(part, place):
        cotangent_copy(part).wait()
        ops_copy(part).wait()
        for b in range(group):
            for k in range(b * span // group, (b + 1) * span // group):
                choose(part * span + k, 0)
            for q in range(share):
                i = (part * group + b) * share + q
                tile = masked_basis(wide_ref, count_ref, i).astype(BF)
                grad_ref[i] = dot(tile, cotangent_ref[i]).astype(BF)
                for p in range(q * slots, (q + 1) * slots):
                    code = code_ref[part * group + b, p]
                    list_ref[place] = code
                    place += 1 + (code >> 31)
            list_ref[place] = dummy
            place = ((place + 1) >> 1) << 1
        return place

    place = lax.fori_loop(0, parts, moments, 0)
    for q in range(2 * UNROLL):
        list_ref[place + q] = dummy
    turns = (place + 2 * UNROLL - 1) // (2 * UNROLL)
    rest_copy.wait()
    for k in range(parts * span, coeffs):
        choose(k, 0)

    def prepare(b, carry):
        wide = rows_ref[pl.ds(b, ROWS, stride=batches), :]
        op_ref[b] = wide.astype(BF)
        back_op_ref[b] = jnp.pad(wide, ((0, 128 - ROWS), (0, 0))).T[:ROWS].astype(BF)
        return carry

    lax.fori_loop(0, batches, prepare, 0, unroll=4)
    op_copy = pltpu.make_async_copy(op_ref, op_hbm, sems.at[parts])
    op_copy.start()

    def turn(j, carry):
        for q in range(UNROLL):
            d = 2 * (j * UNROLL + q)
            b, e0, t0 = decode(list_ref[d])
            _, e1, t1 = decode(list_ref[d + 1])
            result = dot(back_op_ref[b][:, :ROWS], jnp.concatenate([grad_ref[t0], grad_ref[t1]], axis=1))
            total_ref[e0] += result[:, :128]
            total_ref[e1] += result[:, 128:]
        return carry

    lax.fori_loop(0, turns, turn, 0)
    row = lax.broadcasted_iota(I32, (ROWS - MAIN, 128), 0)
    packed = flat(back_ref)

    def narrow(s, carry):
        tail = jnp.where(row == 1, fetch_ref[0, s].astype(F32), total_ref[s, MAIN:, :])
        tile = jnp.concatenate([total_ref[s, :MAIN, :], tail], axis=0).astype(BF)
        packed[block(s), :] = tile[:KEEP]
        return carry

    pieces = 8
    width = remote // pieces

    def send(part):
        rows = pl.ds(part * width, width)
        return pltpu.make_async_copy(back_ref.at[rows], back_hbm.at[rows], out_sems.at[part])

    def ship(part, carry):
        for q in range(width):
            narrow(part * width + q, 0)
        send(part).start()
        return carry

    lax.fori_loop(0, pieces, ship, 0)
    op_copy.wait()
    for part in range(pieces):
        send(part).wait()


def beside_kernel(
    count_ref,
    target_ref,
    source_ref,
    fill_ref,
    charges_hbm,
    cotangent_hbm,
    basis_hbm,
    op_ref,
    mult_hbm,
    local_ref,
    own_ref,
    atoms_ref,
    list_ref,
    charges_ref,
    cotangent_ref,
    basis_ref,
    wide_ref,
    mult_ref,
    packed_ref,
    grad_ref,
    back_op_ref,
    own_target,
    own_source,
    sems,
):
    cells = mult_ref.shape[0]
    batches = op_ref.shape[0]
    copies = [
        pltpu.make_async_copy(src, dst, sems.at[k])
        for k, (src, dst) in enumerate(
            ((basis_hbm, basis_ref), (charges_hbm, charges_ref), (cotangent_hbm, cotangent_ref))
        )
    ]
    for copy in copies:
        copy.start()
    clear(local_ref, cells)
    clear(own_ref, cells)
    for copy in copies:
        copy.wait()
    spread_basis(basis_ref, wide_ref)
    packed = flat(packed_ref)

    def turn(i, carry):
        tile = masked_basis(wide_ref, count_ref, i)
        both = jnp.concatenate([charges_ref[i], cotangent_ref[i]], axis=1)
        result = dot(tile.astype(BF), both).astype(BF)
        mult_ref[i] = result[:, :128]
        packed[block(i), :] = result[:KEEP, :128]
        grad_ref[i] = result[:, 128:]
        atoms_ref[i] = jnp.pad(tile, ((0, 128 - ROWS), (0, 0))).T.astype(BF)
        return carry

    lax.fori_loop(0, cells, turn, 0, unroll=4)
    mult_copy = pltpu.make_async_copy(packed_ref, mult_hbm, sems.at[0])
    mult_copy.start()

    def prepare(b, carry):
        wide = jnp.pad(op_ref[b].astype(F32), ((0, 128 - ROWS), (0, 0)))
        back_op_ref[b] = wide.T[:ROWS].astype(BF)
        return carry

    lax.fori_loop(0, batches, prepare, 0, unroll=2)
    dummy = encode(0, 0, cells)

    def batch(b, place):
        fill = fill_ref[b]

        def sort(p, places):
            own, far = places
            entry = source_ref[b, p] - cells
            target = target_ref[b, p]
            is_far = entry >= 0

            @pl.when(is_far)
            def _():
                list_ref[far] = encode(b, entry, target)

            @pl.when(jnp.logical_not(is_far))
            def _():
                own_target[own] = target
                own_source[own] = entry + cells

            step = is_far.astype(I32)
            return own + 1 - step, far + step

        own, far = lax.fori_loop(0, fill, sort, (0, place))
        list_ref[far] = dummy
        for q in range(8):
            own_target[own + q] = cells
            own_source[own + q] = cells
        op = op_ref[b][:, :ROWS]
        back_op = back_op_ref[b][:, :ROWS]

        def chunk(j, carry):
            for q in range(0, 8, 2):
                t0, t1 = own_target[j * 8 + q], own_target[j * 8 + q + 1]
                e0, e1 = own_source[j * 8 + q], own_source[j * 8 + q + 1]
                result = dot(op, jnp.concatenate([mult_ref[jnp.minimum(e0, cells - 1)], mult_ref[jnp.minimum(e1, cells - 1)]], axis=1))
                local_ref[t0] += result[:, :128]
                local_ref[t1] += result[:, 128:]
                result = dot(back_op, jnp.concatenate([grad_ref[jnp.minimum(t0, cells - 1)], grad_ref[jnp.minimum(t1, cells - 1)]], axis=1))
                own_ref[e0] += result[:, :128]
                own_ref[e1] += result[:, 128:]
            return carry

        lax.fori_loop(0, (own + 7) // 8, chunk, 0)
        return ((far + 1) // 2) * 2

    place = lax.fori_loop(0, batches, batch, 2)
    for q in range(2 * UNROLL):
        list_ref[place + q] = dummy
    list_ref[0] = (place - 2 + 2 * UNROLL - 1) // (2 * UNROLL)
    list_ref[1] = 0
    mult_copy.wait()


def pack_kernel(mult_hbm, back_hbm, out_hbm, asked_ref, mult_ref, tail_ref, wish_ref, sems):
    remote = back_hbm.shape[0]
    tail_copy = pltpu.make_async_copy(back_hbm.at[:, pl.ds(MAIN // 2, 1)], tail_ref, sems.at[0])
    tail_copy.start()
    mult_copy = pltpu.make_async_copy(mult_hbm, mult_ref, sems.at[1])
    mult_copy.start()
    row = lax.broadcasted_iota(I32, (16, 128), 0)
    lane = lax.broadcasted_iota(I32, (16, 128), 1)
    tails = tail_ref.reshape(2 * remote, 128)
    tail_copy.wait()
    wish = jnp.zeros((16, 128), F32)
    for g in range(remote // 8):
        tile = tails[16 * g : 16 * g + 16, :].astype(F32)
        wish = jnp.where(row == 2 * (lane - 8 * g) + 1, tile, wish)
    wish_ref[...] = jnp.sum(wish, axis=0, keepdims=True).astype(I32)
    wish_copy = pltpu.make_async_copy(wish_ref, asked_ref, sems.at[2])
    wish_copy.start()
    mult_copy.wait()
    wish_copy.wait()

    def one(s, carry):
        pltpu.make_async_copy(mult_ref.at[asked_ref[0, s]], out_hbm.at[s], sems.at[3]).start()
        return carry

    lax.fori_loop(0, remote, one, 0, unroll=8)
    pltpu.make_async_copy(back_hbm, out_hbm, sems.at[3]).wait()


def charge_kernel(asked_ref, returned_hbm, own_hbm, atoms_hbm, charge_hbm, returned_ref, own_ref, atoms_ref, charge_ref, sems):
    cells = charge_ref.shape[0]
    remote = returned_ref.shape[0]
    copies = [
        pltpu.make_async_copy(src, dst, sems.at[k])
        for k, (src, dst) in enumerate(((own_hbm, own_ref), (returned_hbm, returned_ref), (atoms_hbm, atoms_ref)))
    ]
    for copy in copies:
        copy.start()
    for copy in copies:
        copy.wait()
    packed = flat(returned_ref)

    def collect(s, carry):
        own_ref[asked_ref[0, s], :KEEP, :] += packed[block(s), :].astype(F32)
        return carry

    lax.fori_loop(0, remote, collect, 0, unroll=4)
    row = lax.broadcasted_iota(I32, (ROWS, 128), 0)

    def atoms(i, carry):
        grads = jnp.where(row > MAIN, 0.0, own_ref[i]).astype(BF)
        charge_ref[i] = dot(atoms_ref[i][:, :ROWS], grads).astype(BF)
        return carry

    lax.fori_loop(0, cells, atoms, 0, unroll=4)
    out = pltpu.make_async_copy(charge_ref, charge_hbm, sems.at[0])
    out.start()
    out.wait()


def far_kernel(
    list_ref,
    incoming_hbm,
    local_hbm,
    atoms_hbm,
    op_hbm,
    potential_hbm,
    incoming_ref,
    local_ref,
    atoms_ref,
    op_ref,
    sum_ref,
    potential_ref,
    sems,
    out_sems,
):
    cells = atoms_ref.shape[0]
    copies = [
        pltpu.make_async_copy(src, dst, sems.at[k])
        for k, (src, dst) in enumerate(
            ((op_hbm, op_ref), (incoming_hbm, incoming_ref), (local_hbm, local_ref), (atoms_hbm, atoms_ref))
        )
    ]
    for copy in copies:
        copy.start()
    clear(sum_ref, cells)
    packed = flat(incoming_ref)
    for copy in copies[:2]:
        copy.wait()

    def turn(j, carry):
        for q in range(UNROLL):
            d = 2 * (j * UNROLL + q + 1)
            b, e0, t0 = decode(list_ref[d])
            _, e1, t1 = decode(list_ref[d + 1])
            both = jnp.concatenate([packed[block(e0), :], packed[block(e1), :]], axis=1)
            result = dot(op_ref[b][:, :KEEP], both)
            sum_ref[t0] += result[:, :128]
            sum_ref[t1] += result[:, 128:]
        return carry

    lax.fori_loop(0, list_ref[0], turn, 0)
    for copy in copies[2:]:
        copy.wait()

    def atoms(i, carry):
        whole = (sum_ref[i] + local_ref[i]).astype(BF)
        potential_ref[i] = dot(atoms_ref[i][:, :ROWS], whole).astype(BF)
        return carry

    outs = []
    parts = 4
    width = cells // parts
    for part in range(parts):
        lax.fori_loop(part * width, (part + 1) * width, atoms, 0, unroll=16)
        rows = pl.ds(part * width, width)
        copy = pltpu.make_async_copy(potential_ref.at[rows], potential_hbm.at[rows], out_sems.at[part])
        copy.start()
        outs.append(copy)
    for copy in outs:
        copy.wait()


SMEM = pl.BlockSpec(memory_space=pltpu.SMEM)
VMEM = pl.BlockSpec(memory_space=pltpu.VMEM)
ANY = pl.BlockSpec(memory_space=pl.ANY)
Shape = jax.ShapeDtypeStruct


def call_back(leaf_count, fill, wishes, batch_class, targets, sources, cotangent, basis_major, ops_major):
    coeffs, cells, slots = basis_major.shape
    domains = wishes.shape[1]
    batches, batch_size = targets.shape
    channels = cotangent.shape[2]
    return pl.pallas_call(
        back_kernel,
        out_shape=(
            Shape((domains, KEEP // 2, 2, channels), BF),
            Shape((batches, ROWS, 128), BF),
        ),
        in_specs=[SMEM] * 4 + [VMEM] * 2 + [ANY] * 3,
        out_specs=(ANY, ANY),
        scratch_shapes=[
            pltpu.VMEM((cells, slots, channels), BF),
            pltpu.VMEM((coeffs, cells, slots), BF),
            pltpu.VMEM(ops_major.shape, BF),
            pltpu.VMEM((ROWS * STRIDE, slots), F32),
            pltpu.VMEM((ROWS * batches, 128), F32),
            pltpu.VMEM((cells, ROWS, channels), BF),
            pltpu.VMEM((domains + 1, ROWS, channels), F32),
            pltpu.VMEM((domains, KEEP // 2, 2, channels), BF),
            pltpu.VMEM((batches, ROWS, 128), BF),
            pltpu.VMEM((batches, ROWS, 128), BF),
            pltpu.VMEM((batches, batch_size), I32),
            pltpu.SMEM((batches, batch_size), I32),
            pltpu.SMEM((batches * batch_size + 2 * UNROLL + 2,), I32),
            pltpu.SemaphoreType.DMA((6,)),
            pltpu.SemaphoreType.DMA((5,)),
            pltpu.SemaphoreType.DMA((8,)),
        ],
        compiler_params=params(),
        name="back_pairs",
    )(leaf_count, fill, wishes, batch_class, targets, sources, cotangent, basis_major, ops_major)


def call_beside(leaf_count, targets, sources, fill, charges, cotangent, basis_major, ops):
    coeffs, cells, slots = basis_major.shape
    batches, batch_size = targets.shape
    channels = charges.shape[2]
    return pl.pallas_call(
        beside_kernel,
        out_shape=(
            Shape((cells, KEEP // 2, 2, channels), BF),
            Shape((cells + 1, ROWS, channels), F32),
            Shape((cells + 1, ROWS, channels), F32),
            Shape((cells, slots, 128), BF),
            Shape((batches * batch_size + 2 * UNROLL + 4,), I32),
        ),
        in_specs=[SMEM] * 4 + [ANY] * 3 + [VMEM],
        out_specs=(ANY, VMEM, VMEM, VMEM, SMEM),
        scratch_shapes=[
            pltpu.VMEM((cells, slots, channels), BF),
            pltpu.VMEM((cells, slots, channels), BF),
            pltpu.VMEM((coeffs, cells, slots), BF),
            pltpu.VMEM((ROWS * STRIDE, slots), F32),
            pltpu.VMEM((cells, ROWS, channels), BF),
            pltpu.VMEM((cells, KEEP // 2, 2, channels), BF),
            pltpu.VMEM((cells, ROWS, channels), BF),
            pltpu.VMEM((batches, ROWS, 128), BF),
            pltpu.SMEM((batch_size + 8,), I32),
            pltpu.SMEM((batch_size + 8,), I32),
            pltpu.SemaphoreType.DMA((3,)),
        ],
        compiler_params=params(),
        cost_estimate=pl.CostEstimate(flops=400_000_000, bytes_accessed=8_000_000, transcendentals=0),
        name="own_pairs",
    )(leaf_count, targets, sources, fill, charges, cotangent, basis_major, ops)


def call_pack(mult, returned):
    cells, _, _, channels = mult.shape
    domains = returned.shape[0]
    return pl.pallas_call(
        pack_kernel,
        out_shape=(Shape(returned.shape, BF), Shape((1, domains), I32)),
        in_specs=[ANY] * 2,
        out_specs=(ANY, SMEM),
        scratch_shapes=[
            pltpu.VMEM(mult.shape, BF),
            pltpu.VMEM((domains, 1, 2, channels), BF),
            pltpu.VMEM((1, domains), I32),
            pltpu.SemaphoreType.DMA((4,)),
        ],
        compiler_params=params(),
        name="pack_blocks",
    )(mult, returned)


def call_charge(asked, returned, own, atoms):
    cells, slots, _ = atoms.shape
    channels = returned.shape[3]
    return pl.pallas_call(
        charge_kernel,
        out_shape=Shape((cells, slots, channels), BF),
        in_specs=[SMEM] + [ANY] * 3,
        out_specs=ANY,
        scratch_shapes=[
            pltpu.VMEM(returned.shape, BF),
            pltpu.VMEM(own.shape, F32),
            pltpu.VMEM((cells, slots, 128), BF),
            pltpu.VMEM((cells, slots, channels), BF),
            pltpu.SemaphoreType.DMA((3,)),
        ],
        compiler_params=params(),
        cost_estimate=pl.CostEstimate(flops=200_000_000, bytes_accessed=8_000_000, transcendentals=0),
        name="charge_atoms",
    )(asked, returned, own, atoms)


def call_far(pairs, incoming, local_part, atoms, ops):
    cells, slots, _ = atoms.shape
    channels = incoming.shape[3]
    return pl.pallas_call(
        far_kernel,
        out_shape=Shape((cells, slots, channels), BF),
        in_specs=[SMEM] + [ANY] * 4,
        out_specs=ANY,
        scratch_shapes=[
            pltpu.VMEM(incoming.shape, BF),
            pltpu.VMEM(local_part.shape, F32),
            pltpu.VMEM((cells, slots, 128), BF),
            pltpu.VMEM(ops.shape, BF),
            pltpu.VMEM((cells + 1, ROWS, channels), F32),
            pltpu.VMEM((cells, slots, channels), BF),
            pltpu.SemaphoreType.DMA((4,)),
            pltpu.SemaphoreType.DMA((4,)),
        ],
        compiler_params=params(),
        name="far_pairs_atoms",
    )(pairs, incoming, local_part, atoms, ops)


def local(
    charges,
    basis,
    leaf_count,
    cotangent,
    m2l_ops,
    fetch_cells,
    pair_target,
    pair_source,
    batch_class,
    batch_fill,
):
    basis_major = basis.transpose(1, 0, 2)
    wishes = fetch_cells.reshape(1, -1)
    targets, sources, fill = pair_target[0], pair_source[0], batch_fill[0]
    back, ops = call_back(
        leaf_count, fill, wishes, batch_class[0], targets, sources, cotangent, basis_major, m2l_ops.transpose(1, 2, 0)
    )
    returned = lax.all_to_all(back, ("dx", "dy"), split_axis=0, concat_axis=0, tiled=True)
    mult, local_part, own, atoms, pairs = call_beside(
        leaf_count, targets, sources, fill, charges, cotangent, basis_major, ops
    )
    outgoing, asked = call_pack(mult, returned)
    incoming = lax.all_to_all(outgoing, ("dx", "dy"), split_axis=0, concat_axis=0, tiled=True)
    charge_grad = call_charge(asked, returned, own, atoms)
    potential = call_far(pairs, incoming, local_part, atoms, ops)
    return potential, charge_grad


def solution(mesh):
    in_specs = (
        P(("dx", "dy"), None, None),
        P(("dx", "dy"), None, None),
        P(("dx", "dy")),
        P(("dx", "dy"), None, None),
        P(),
        P(("dx", "dy"), None, None),
        P(("dx", "dy"), None, None),
        P(("dx", "dy"), None, None),
        P(("dx", "dy"), None),
        P(("dx", "dy"), None),
    )
    out_specs = (P(("dx", "dy"), None, None), P(("dx", "dy"), None, None))
    return jax.shard_map(local, mesh=mesh, in_specs=in_specs, out_specs=out_specs, check_vma=False)
```

```python
import jax
import jax.numpy as jnp
from jax import lax
from jax.experimental import pallas as pl
from jax.experimental.pallas import tpu as pltpu
from jax.sharding import PartitionSpec as P

BF = jnp.bfloat16
F32 = jnp.float32
I32 = jnp.int32
ROWS = 88
MAIN = 80
KEEP = 82
STRIDE = 72
UNROLL = 16
LIMIT = 62


def dot(a, b):
    return lax.dot_general(a, b, (((1,), (0,)), ((), ())), preferred_element_type=F32)


def params(mib=LIMIT):
    return pltpu.CompilerParams(vmem_limit_bytes=mib << 20)


def flat(ref):
    return ref.reshape(ref.shape[0] * KEEP, ref.shape[-1])


def block(index):
    return pl.ds(pl.multiple_of(index * KEEP, 2), KEEP)


def spread_basis(basis_ref, wide_ref):
    coeffs, cells, slots = basis_ref.shape

    def put(k, carry):
        wide_ref[pl.ds(pl.multiple_of(k * STRIDE, 8), cells), :] = basis_ref[k].astype(F32)
        return carry

    lax.fori_loop(0, coeffs, put, 0, unroll=9)
    wide_ref[coeffs * STRIDE :, :] = jnp.zeros(((ROWS - coeffs) * STRIDE, slots), F32)


def masked_basis(wide_ref, count_ref, cell):
    tile = wide_ref[pl.ds(cell, ROWS, stride=STRIDE), :]
    lane = lax.broadcasted_iota(I32, tile.shape, 1)
    return jnp.where(lane < count_ref[cell], tile, 0.0)


class Split:
    def __init__(self, src, dst, sem, pieces):
        self.src, self.dst, self.sem, self.pieces = src, dst, sem, pieces

    def start(self):
        size = self.src.shape[0]
        edges = [size * k // self.pieces for k in range(self.pieces + 1)]
        for low, high in zip(edges, edges[1:]):
            rows = pl.ds(low, high - low)
            pltpu.make_async_copy(self.src.at[rows], self.dst.at[rows], self.sem).start()

    def wait(self):
        pltpu.make_async_copy(self.src, self.dst, self.sem).wait()


def clear(ref, count):
    def one(e, carry):
        ref[e] = jnp.zeros(ref.shape[1:], ref.dtype)
        return carry

    lax.fori_loop(0, count, one, 0, unroll=8)


def encode(batch, entry, target):
    return batch * 65536 + entry * 256 + target


def decode(code):
    return code >> 16, (code >> 8) & 255, code & 255


def choose_operators(class_ref, ops_ref, rows_ref):
    coeffs, _, classes = ops_ref.shape
    batches = rows_ref.shape[0] // ROWS
    rows_ref[...] = jnp.zeros(rows_ref.shape, F32)
    row = lax.broadcasted_iota(I32, (batches, classes), 0)
    wanted = jnp.zeros((batches, classes), I32)
    for b in range(batches):
        wanted = jnp.where(row == b, class_ref[b], wanted)
    hot = (wanted == lax.broadcasted_iota(I32, (batches, classes), 1)).astype(F32).astype(BF)

    def one(k, carry):
        picked = lax.dot_general(hot, ops_ref[k], (((1,), (1,)), ((), ())), preferred_element_type=F32)
        rows_ref[pl.ds(pl.multiple_of(k * batches, batches), batches), :coeffs] = picked
        return carry

    return one


def back_kernel(
    count_hbm,
    fill_hbm,
    fetch_hbm,
    class_hbm,
    target_hbm,
    source_hbm,
    cotangent_hbm,
    basis_hbm,
    ops_hbm,
    back_hbm,
    op_hbm,
    count_ref,
    fill_ref,
    fetch_ref,
    class_ref,
    target_ref,
    source_ref,
    cotangent_ref,
    basis_ref,
    ops_ref,
    wide_ref,
    rows_ref,
    grad_ref,
    total_ref,
    back_ref,
    op_ref,
    back_op_ref,
    found_ref,
    code_ref,
    list_ref,
    small_sems,
    sems,
    ops_sems,
    out_sems,
):
    cells = cotangent_ref.shape[0]
    coeffs = basis_ref.shape[0]
    batches, batch_size = target_ref.shape
    small_copies = [
        pltpu.make_async_copy(src, dst, small_sems.at[k])
        for k, (src, dst) in enumerate(
            (
                (fill_hbm, fill_ref),
                (target_hbm, target_ref),
                (source_hbm, source_ref),
                (class_hbm, class_ref),
                (count_hbm, count_ref),
                (fetch_hbm, fetch_ref),
            )
        )
    ]
    remote = back_ref.shape[0]
    parts = 4
    step = cells // parts
    span = coeffs // parts
    basis_copy = Split(basis_hbm, basis_ref, sems.at[parts], 9)
    basis_copy.start()
    for copy in small_copies:
        copy.start()

    def cotangent_copy(part):
        rows = pl.ds(part * step, step)
        return pltpu.make_async_copy(cotangent_hbm.at[rows], cotangent_ref.at[rows], sems.at[part])

    def ops_copy(part):
        rows = pl.ds(part * span, span)
        return pltpu.make_async_copy(ops_hbm.at[rows], ops_ref.at[rows], ops_sems.at[part])

    for part in range(parts):
        cotangent_copy(part).start()
        ops_copy(part).start()
    rows = pl.ds(parts * span, coeffs - parts * span)
    rest_copy = pltpu.make_async_copy(ops_hbm.at[rows], ops_ref.at[rows], ops_sems.at[parts])
    rest_copy.start()
    clear(total_ref, remote)
    for copy in small_copies:
        copy.wait()

    batch = lax.broadcasted_iota(I32, (batches, batch_size), 0)
    slot = lax.broadcasted_iota(I32, (batches, batch_size), 1)
    fill = jnp.zeros((batches, batch_size), I32)
    for b in range(batches):
        fill = jnp.where(batch == b, fill_ref[b], fill)
    entry = source_ref[...] - cells
    far = (slot < fill) & (entry >= 0)
    found_ref[...] = jnp.where(far, encode(batch, entry, target_ref[...]), -1)
    code_copy = pltpu.make_async_copy(found_ref, code_ref, sems.at[parts + 1])
    code_copy.start()
    choose = choose_operators(class_ref, ops_ref, rows_ref)
    basis_copy.wait()
    spread_basis(basis_ref, wide_ref)
    code_copy.wait()

    share = cells // batches
    slots = batch_size // share
    dummy = encode(0, remote, 0)
    group = batches // parts

    def moments(part, place):
        cotangent_copy(part).wait()
        ops_copy(part).wait()
        for b in range(group):
            for k in range(b * span // group, (b + 1) * span // group):
                choose(part * span + k, 0)
            for q in range(share):
                i = (part * group + b) * share + q
                tile = masked_basis(wide_ref, count_ref, i).astype(BF)
                grad_ref[i] = dot(tile, cotangent_ref[i]).astype(BF)
                for p in range(q * slots, (q + 1) * slots):
                    code = code_ref[part * group + b, p]
                    list_ref[place] = code
                    place += 1 + (code >> 31)
            list_ref[place] = dummy
            place = ((place + 1) >> 1) << 1
        return place

    place = lax.fori_loop(0, parts, moments, 0)
    for q in range(2 * UNROLL):
        list_ref[place + q] = dummy
    turns = (place + 2 * UNROLL - 1) // (2 * UNROLL)
    rest_copy.wait()
    for k in range(parts * span, coeffs):
        choose(k, 0)

    def prepare(b, carry):
        wide = rows_ref[pl.ds(b, ROWS, stride=batches), :]
        op_ref[b] = wide.astype(BF)
        back_op_ref[b] = jnp.pad(wide, ((0, 128 - ROWS), (0, 0))).T[:ROWS].astype(BF)
        return carry

    lax.fori_loop(0, batches, prepare, 0, unroll=4)
    op_copy = pltpu.make_async_copy(op_ref, op_hbm, sems.at[parts])
    op_copy.start()

    def turn(j, carry):
        for q in range(UNROLL):
            d = 2 * (j * UNROLL + q)
            b, e0, t0 = decode(list_ref[d])
            _, e1, t1 = decode(list_ref[d + 1])
            result = dot(back_op_ref[b][:, :ROWS], jnp.concatenate([grad_ref[t0], grad_ref[t1]], axis=1))
            total_ref[e0] += result[:, :128]
            total_ref[e1] += result[:, 128:]
        return carry

    lax.fori_loop(0, turns, turn, 0)
    row = lax.broadcasted_iota(I32, (ROWS - MAIN, 128), 0)
    packed = flat(back_ref)

    def narrow(s, carry):
        tail = jnp.where(row == 1, fetch_ref[0, s].astype(F32), total_ref[s, MAIN:, :])
        tile = jnp.concatenate([total_ref[s, :MAIN, :], tail], axis=0).astype(BF)
        packed[block(s), :] = tile[:KEEP]
        return carry

    pieces = 8
    width = remote // pieces

    def send(part):
        rows = pl.ds(part * width, width)
        return pltpu.make_async_copy(back_ref.at[rows], back_hbm.at[rows], out_sems.at[part])

    def ship(part, carry):
        for q in range(width):
            narrow(part * width + q, 0)
        send(part).start()
        return carry

    lax.fori_loop(0, pieces, ship, 0)
    op_copy.wait()
    for part in range(pieces):
        send(part).wait()


def beside_kernel(
    count_ref,
    target_ref,
    source_ref,
    fill_ref,
    charges_hbm,
    cotangent_hbm,
    basis_hbm,
    op_ref,
    mult_hbm,
    local_ref,
    own_ref,
    atoms_ref,
    list_ref,
    charges_ref,
    cotangent_ref,
    basis_ref,
    wide_ref,
    mult_ref,
    packed_ref,
    grad_ref,
    back_op_ref,
    own_target,
    own_source,
    sems,
):
    cells = mult_ref.shape[0]
    batches = op_ref.shape[0]
    copies = [
        pltpu.make_async_copy(src, dst, sems.at[k])
        for k, (src, dst) in enumerate(
            ((basis_hbm, basis_ref), (charges_hbm, charges_ref), (cotangent_hbm, cotangent_ref))
        )
    ]
    for copy in copies:
        copy.start()
    clear(local_ref, cells)
    clear(own_ref, cells)
    for copy in copies:
        copy.wait()
    spread_basis(basis_ref, wide_ref)
    packed = flat(packed_ref)

    def turn(i, carry):
        tile = masked_basis(wide_ref, count_ref, i)
        both = jnp.concatenate([charges_ref[i], cotangent_ref[i]], axis=1)
        result = dot(tile.astype(BF), both).astype(BF)
        mult_ref[i] = result[:, :128]
        packed[block(i), :] = result[:KEEP, :128]
        grad_ref[i] = result[:, 128:]
        atoms_ref[i] = jnp.pad(tile, ((0, 128 - ROWS), (0, 0))).T.astype(BF)
        return carry

    lax.fori_loop(0, cells, turn, 0, unroll=4)
    mult_copy = pltpu.make_async_copy(packed_ref, mult_hbm, sems.at[0])
    mult_copy.start()

    def prepare(b, carry):
        wide = jnp.pad(op_ref[b].astype(F32), ((0, 128 - ROWS), (0, 0)))
        back_op_ref[b] = wide.T[:ROWS].astype(BF)
        return carry

    lax.fori_loop(0, batches, prepare, 0, unroll=2)
    dummy = encode(0, 0, cells)

    def batch(b, place):
        fill = fill_ref[b]

        def sort(p, places):
            own, far = places
            entry = source_ref[b, p] - cells
            target = target_ref[b, p]
            is_far = entry >= 0

            @pl.when(is_far)
            def _():
                list_ref[far] = encode(b, entry, target)

            @pl.when(jnp.logical_not(is_far))
            def _():
                own_target[own] = target
                own_source[own] = entry + cells

            step = is_far.astype(I32)
            return own + 1 - step, far + step

        own, far = lax.fori_loop(0, fill, sort, (0, place))
        list_ref[far] = dummy
        for q in range(8):
            own_target[own + q] = cells
            own_source[own + q] = cells
        op = op_ref[b][:, :ROWS]
        back_op = back_op_ref[b][:, :ROWS]

        def chunk(j, carry):
            for q in range(0, 8, 2):
                t0, t1 = own_target[j * 8 + q], own_target[j * 8 + q + 1]
                e0, e1 = own_source[j * 8 + q], own_source[j * 8 + q + 1]
                result = dot(op, jnp.concatenate([mult_ref[jnp.minimum(e0, cells - 1)], mult_ref[jnp.minimum(e1, cells - 1)]], axis=1))
                local_ref[t0] += result[:, :128]
                local_ref[t1] += result[:, 128:]
                result = dot(back_op, jnp.concatenate([grad_ref[jnp.minimum(t0, cells - 1)], grad_ref[jnp.minimum(t1, cells - 1)]], axis=1))
                own_ref[e0] += result[:, :128]
                own_ref[e1] += result[:, 128:]
            return carry

        lax.fori_loop(0, (own + 7) // 8, chunk, 0)
        return ((far + 1) // 2) * 2

    place = lax.fori_loop(0, batches, batch, 2)
    for q in range(2 * UNROLL):
        list_ref[place + q] = dummy
    list_ref[0] = (place - 2 + 2 * UNROLL - 1) // (2 * UNROLL)
    list_ref[1] = 0
    mult_copy.wait()


def pack_kernel(mult_hbm, back_hbm, out_hbm, asked_ref, mult_ref, tail_ref, wish_ref, sems):
    remote = back_hbm.shape[0]
    tail_copy = pltpu.make_async_copy(back_hbm.at[:, pl.ds(MAIN // 2, 1)], tail_ref, sems.at[0])
    tail_copy.start()
    mult_copy = Split(mult_hbm, mult_ref, sems.at[1], 8)
    mult_copy.start()
    row = lax.broadcasted_iota(I32, (16, 128), 0)
    lane = lax.broadcasted_iota(I32, (16, 128), 1)
    tails = tail_ref.reshape(2 * remote, 128)
    tail_copy.wait()
    wish = jnp.zeros((16, 128), F32)
    for g in range(remote // 8):
        tile = tails[16 * g : 16 * g + 16, :].astype(F32)
        wish = jnp.where(row == 2 * (lane - 8 * g) + 1, tile, wish)
    wish_ref[...] = jnp.sum(wish, axis=0, keepdims=True).astype(I32)
    wish_copy = pltpu.make_async_copy(wish_ref, asked_ref, sems.at[2])
    wish_copy.start()
    mult_copy.wait()
    wish_copy.wait()

    def one(s, carry):
        pltpu.make_async_copy(mult_ref.at[asked_ref[0, s]], out_hbm.at[s], sems.at[3]).start()
        return carry

    lax.fori_loop(0, remote, one, 0, unroll=8)
    pltpu.make_async_copy(back_hbm, out_hbm, sems.at[3]).wait()


def charge_kernel(asked_ref, returned_hbm, own_hbm, atoms_hbm, charge_hbm, returned_ref, own_ref, atoms_ref, charge_ref, sems):
    cells = charge_ref.shape[0]
    remote = returned_ref.shape[0]
    copies = [
        pltpu.make_async_copy(src, dst, sems.at[k])
        for k, (src, dst) in enumerate(((own_hbm, own_ref), (returned_hbm, returned_ref), (atoms_hbm, atoms_ref)))
    ]
    for copy in copies:
        copy.start()
    for copy in copies:
        copy.wait()
    packed = flat(returned_ref)

    def collect(s, carry):
        own_ref[asked_ref[0, s], :KEEP, :] += packed[block(s), :].astype(F32)
        return carry

    lax.fori_loop(0, remote, collect, 0, unroll=4)
    row = lax.broadcasted_iota(I32, (ROWS, 128), 0)

    def atoms(i, carry):
        grads = jnp.where(row > MAIN, 0.0, own_ref[i]).astype(BF)
        charge_ref[i] = dot(atoms_ref[i][:, :ROWS], grads).astype(BF)
        return carry

    lax.fori_loop(0, cells, atoms, 0, unroll=4)
    out = pltpu.make_async_copy(charge_ref, charge_hbm, sems.at[0])
    out.start()
    out.wait()


def far_kernel(
    list_hbm,
    incoming_ref,
    local_hbm,
    atoms_hbm,
    op_hbm,
    potential_hbm,
    list_ref,
    local_ref,
    atoms_ref,
    op_ref,
    sum_ref,
    potential_ref,
    sems,
    out_sems,
):
    cells = atoms_ref.shape[0]
    copies = [
        Split(src, dst, sems.at[k], pieces)
        for k, (src, dst, pieces) in enumerate(
            (
                (list_hbm, list_ref, 1),
                (op_hbm, op_ref, 2),
                (atoms_hbm, atoms_ref, 4),
                (local_hbm, local_ref, 5),
            )
        )
    ]
    for copy in copies:
        copy.start()
    clear(sum_ref, cells)
    packed = flat(incoming_ref)
    for copy in copies[:2]:
        copy.wait()

    def turn(j, carry):
        for q in range(UNROLL):
            d = 2 * (j * UNROLL + q + 1)
            b, e0, t0 = decode(list_ref[d])
            _, e1, t1 = decode(list_ref[d + 1])
            both = jnp.concatenate([packed[block(e0), :], packed[block(e1), :]], axis=1)
            result = dot(op_ref[b][:, :KEEP], both)
            sum_ref[t0] += result[:, :128]
            sum_ref[t1] += result[:, 128:]
        return carry

    lax.fori_loop(0, list_ref[0], turn, 0)
    for copy in copies[2:]:
        copy.wait()

    def atoms(i, carry):
        whole = (sum_ref[i] + local_ref[i]).astype(BF)
        potential_ref[i] = dot(atoms_ref[i][:, :ROWS], whole).astype(BF)
        return carry

    outs = []
    parts = 8
    width = cells // parts
    for part in range(parts):
        lax.fori_loop(part * width, (part + 1) * width, atoms, 0, unroll=8)
        rows = pl.ds(part * width, width)
        copy = pltpu.make_async_copy(potential_ref.at[rows], potential_hbm.at[rows], out_sems.at[part])
        copy.start()
        outs.append(copy)
    for copy in outs:
        copy.wait()


SMEM = pl.BlockSpec(memory_space=pltpu.SMEM)
VMEM = pl.BlockSpec(memory_space=pltpu.VMEM)
ANY = pl.BlockSpec(memory_space=pl.ANY)
Shape = jax.ShapeDtypeStruct


def call_back(leaf_count, fill, wishes, batch_class, targets, sources, cotangent, basis_major, ops_major):
    coeffs, cells, slots = basis_major.shape
    domains = wishes.shape[1]
    batches, batch_size = targets.shape
    channels = cotangent.shape[2]
    return pl.pallas_call(
        back_kernel,
        out_shape=(
            Shape((domains, KEEP // 2, 2, channels), BF),
            Shape((batches, ROWS, 128), BF),
        ),
        in_specs=[ANY] * 9,
        out_specs=(ANY, ANY),
        scratch_shapes=[
            pltpu.SMEM(leaf_count.shape, I32),
            pltpu.SMEM(fill.shape, I32),
            pltpu.SMEM(wishes.shape, I32),
            pltpu.SMEM(batch_class.shape, I32),
            pltpu.VMEM(targets.shape, I32),
            pltpu.VMEM(sources.shape, I32),
            pltpu.VMEM((cells, slots, channels), BF),
            pltpu.VMEM((coeffs, cells, slots), BF),
            pltpu.VMEM(ops_major.shape, BF),
            pltpu.VMEM((ROWS * STRIDE, slots), F32),
            pltpu.VMEM((ROWS * batches, 128), F32),
            pltpu.VMEM((cells, ROWS, channels), BF),
            pltpu.VMEM((domains + 1, ROWS, channels), F32),
            pltpu.VMEM((domains, KEEP // 2, 2, channels), BF),
            pltpu.VMEM((batches, ROWS, 128), BF),
            pltpu.VMEM((batches, ROWS, 128), BF),
            pltpu.VMEM((batches, batch_size), I32),
            pltpu.SMEM((batches, batch_size), I32),
            pltpu.SMEM((batches * batch_size + 2 * UNROLL + 2,), I32),
            pltpu.SemaphoreType.DMA((6,)),
            pltpu.SemaphoreType.DMA((6,)),
            pltpu.SemaphoreType.DMA((5,)),
            pltpu.SemaphoreType.DMA((8,)),
        ],
        compiler_params=params(),
        name="back_pairs",
    )(leaf_count, fill, wishes, batch_class, targets, sources, cotangent, basis_major, ops_major)


def call_beside(leaf_count, targets, sources, fill, charges, cotangent, basis_major, ops):
    coeffs, cells, slots = basis_major.shape
    batches, batch_size = targets.shape
    channels = charges.shape[2]
    return pl.pallas_call(
        beside_kernel,
        out_shape=(
            Shape((cells, KEEP // 2, 2, channels), BF),
            Shape((cells + 1, ROWS, channels), F32),
            Shape((cells + 1, ROWS, channels), F32),
            Shape((cells, slots, 128), BF),
            Shape((batches * batch_size + 2 * UNROLL + 4,), I32),
        ),
        in_specs=[SMEM] * 4 + [ANY] * 3 + [VMEM],
        out_specs=(ANY, VMEM, VMEM, VMEM, SMEM),
        scratch_shapes=[
            pltpu.VMEM((cells, slots, channels), BF),
            pltpu.VMEM((cells, slots, channels), BF),
            pltpu.VMEM((coeffs, cells, slots), BF),
            pltpu.VMEM((ROWS * STRIDE, slots), F32),
            pltpu.VMEM((cells, ROWS, channels), BF),
            pltpu.VMEM((cells, KEEP // 2, 2, channels), BF),
            pltpu.VMEM((cells, ROWS, channels), BF),
            pltpu.VMEM((batches, ROWS, 128), BF),
            pltpu.SMEM((batch_size + 8,), I32),
            pltpu.SMEM((batch_size + 8,), I32),
            pltpu.SemaphoreType.DMA((3,)),
        ],
        compiler_params=params(),
        cost_estimate=pl.CostEstimate(flops=400_000_000, bytes_accessed=8_000_000, transcendentals=0),
        name="own_pairs",
    )(leaf_count, targets, sources, fill, charges, cotangent, basis_major, ops)


def call_pack(mult, returned):
    cells, _, _, channels = mult.shape
    domains = returned.shape[0]
    return pl.pallas_call(
        pack_kernel,
        out_shape=(Shape(returned.shape, BF), Shape((1, domains), I32)),
        in_specs=[ANY] * 2,
        out_specs=(ANY, SMEM),
        scratch_shapes=[
            pltpu.VMEM(mult.shape, BF),
            pltpu.VMEM((domains, 1, 2, channels), BF),
            pltpu.VMEM((1, domains), I32),
            pltpu.SemaphoreType.DMA((4,)),
        ],
        compiler_params=params(),
        name="pack_blocks",
    )(mult, returned)


def call_charge(asked, returned, own, atoms):
    cells, slots, _ = atoms.shape
    channels = returned.shape[3]
    return pl.pallas_call(
        charge_kernel,
        out_shape=Shape((cells, slots, channels), BF),
        in_specs=[SMEM] + [ANY] * 3,
        out_specs=ANY,
        scratch_shapes=[
            pltpu.VMEM(returned.shape, BF),
            pltpu.VMEM(own.shape, F32),
            pltpu.VMEM((cells, slots, 128), BF),
            pltpu.VMEM((cells, slots, channels), BF),
            pltpu.SemaphoreType.DMA((3,)),
        ],
        compiler_params=params(52),
        cost_estimate=pl.CostEstimate(flops=200_000_000, bytes_accessed=8_000_000, transcendentals=0),
        name="charge_atoms",
    )(asked, returned, own, atoms)


def call_far(pairs, incoming, local_part, atoms, ops):
    cells, slots, _ = atoms.shape
    channels = incoming.shape[3]
    return pl.pallas_call(
        far_kernel,
        out_shape=Shape((cells, slots, channels), BF),
        in_specs=[ANY, VMEM] + [ANY] * 3,
        out_specs=ANY,
        scratch_shapes=[
            pltpu.SMEM(pairs.shape, I32),
            pltpu.VMEM(local_part.shape, F32),
            pltpu.VMEM((cells, slots, 128), BF),
            pltpu.VMEM(ops.shape, BF),
            pltpu.VMEM((cells + 1, ROWS, channels), F32),
            pltpu.VMEM((cells, slots, channels), BF),
            pltpu.SemaphoreType.DMA((5,)),
            pltpu.SemaphoreType.DMA((8,)),
        ],
        compiler_params=params(50),
        name="far_pairs_atoms",
    )(pairs, incoming, local_part, atoms, ops)


def local(
    charges,
    basis,
    leaf_count,
    cotangent,
    m2l_ops,
    fetch_cells,
    pair_target,
    pair_source,
    batch_class,
    batch_fill,
):
    basis_major = basis.transpose(1, 0, 2)
    wishes = fetch_cells.reshape(1, -1)
    targets, sources, fill = pair_target[0], pair_source[0], batch_fill[0]
    back, ops = call_back(
        leaf_count, fill, wishes, batch_class[0], targets, sources, cotangent, basis_major, m2l_ops.transpose(1, 2, 0)
    )
    returned = lax.all_to_all(back, ("dx", "dy"), split_axis=0, concat_axis=0, tiled=True)
    mult, local_part, own, atoms, pairs = call_beside(
        leaf_count, targets, sources, fill, charges, cotangent, basis_major, ops
    )
    outgoing, asked = call_pack(mult, returned)
    incoming = lax.all_to_all(outgoing, ("dx", "dy"), split_axis=0, concat_axis=0, tiled=True)
    charge_grad = call_charge(asked, returned, own, atoms)
    potential = call_far(pairs, incoming, local_part, atoms, ops)
    return potential, charge_grad


def solution(mesh):
    in_specs = (
        P(("dx", "dy"), None, None),
        P(("dx", "dy"), None, None),
        P(("dx", "dy")),
        P(("dx", "dy"), None, None),
        P(),
        P(("dx", "dy"), None, None),
        P(("dx", "dy"), None, None),
        P(("dx", "dy"), None, None),
        P(("dx", "dy"), None),
        P(("dx", "dy"), None),
    )
    out_specs = (P(("dx", "dy"), None, None), P(("dx", "dy"), None, None))
    return jax.shard_map(local, mesh=mesh, in_specs=in_specs, out_specs=out_specs, check_vma=False)
```

```python
import jax
import jax.numpy as jnp
from jax import lax
from jax.experimental import pallas as pl
from jax.experimental.pallas import tpu as pltpu
from jax.sharding import PartitionSpec as P

BF = jnp.bfloat16
F32 = jnp.float32
I32 = jnp.int32
ROWS = 88
MAIN = 80
KEEP = 82
STRIDE = 72
UNROLL = 16
LIMIT = 62


def dot(a, b):
    return lax.dot_general(a, b, (((1,), (0,)), ((), ())), preferred_element_type=F32)


def params(mib=LIMIT):
    return pltpu.CompilerParams(vmem_limit_bytes=mib << 20)


def flat(ref):
    return ref.reshape(ref.shape[0] * KEEP, ref.shape[-1])


def block(index):
    return pl.ds(pl.multiple_of(index * KEEP, 2), KEEP)


def spread_basis(basis_ref, wide_ref):
    coeffs, cells, slots = basis_ref.shape

    def put(k, carry):
        wide_ref[pl.ds(pl.multiple_of(k * STRIDE, 8), cells), :] = basis_ref[k].astype(F32)
        return carry

    lax.fori_loop(0, coeffs, put, 0, unroll=9)
    wide_ref[coeffs * STRIDE :, :] = jnp.zeros(((ROWS - coeffs) * STRIDE, slots), F32)


def masked_basis(wide_ref, count_ref, cell):
    tile = wide_ref[pl.ds(cell, ROWS, stride=STRIDE), :]
    lane = lax.broadcasted_iota(I32, tile.shape, 1)
    return jnp.where(lane < count_ref[cell], tile, 0.0)


class Split:
    def __init__(self, src, dst, sem, pieces):
        self.src, self.dst, self.sem, self.pieces = src, dst, sem, pieces

    def start(self):
        size = self.src.shape[0]
        edges = [size * k // self.pieces for k in range(self.pieces + 1)]
        for low, high in zip(edges, edges[1:]):
            rows = pl.ds(low, high - low)
            pltpu.make_async_copy(self.src.at[rows], self.dst.at[rows], self.sem).start()

    def wait(self):
        pltpu.make_async_copy(self.src, self.dst, self.sem).wait()


def clear(ref, count):
    def one(e, carry):
        ref[e] = jnp.zeros(ref.shape[1:], ref.dtype)
        return carry

    lax.fori_loop(0, count, one, 0, unroll=8)


def encode(batch, entry, target):
    return batch * 65536 + entry * 256 + target


def decode(code):
    return code >> 16, (code >> 8) & 255, code & 255


def choose_operators(class_ref, ops_ref, rows_ref):
    coeffs, _, classes = ops_ref.shape
    batches = rows_ref.shape[0] // ROWS
    rows_ref[...] = jnp.zeros(rows_ref.shape, F32)
    row = lax.broadcasted_iota(I32, (batches, classes), 0)
    wanted = jnp.zeros((batches, classes), I32)
    for b in range(batches):
        wanted = jnp.where(row == b, class_ref[b], wanted)
    hot = (wanted == lax.broadcasted_iota(I32, (batches, classes), 1)).astype(F32).astype(BF)

    def one(k, carry):
        picked = lax.dot_general(hot, ops_ref[k], (((1,), (1,)), ((), ())), preferred_element_type=F32)
        rows_ref[pl.ds(pl.multiple_of(k * batches, batches), batches), :coeffs] = picked
        return carry

    return one


def back_kernel(
    count_hbm,
    fill_hbm,
    fetch_hbm,
    class_hbm,
    target_hbm,
    source_hbm,
    cotangent_hbm,
    basis_hbm,
    ops_hbm,
    back_hbm,
    op_hbm,
    count_ref,
    fill_ref,
    fetch_ref,
    class_ref,
    target_ref,
    source_ref,
    cotangent_ref,
    basis_ref,
    ops_ref,
    wide_ref,
    rows_ref,
    grad_ref,
    total_ref,
    back_ref,
    op_ref,
    back_op_ref,
    found_ref,
    code_ref,
    list_ref,
    small_sems,
    sems,
    ops_sems,
    out_sems,
):
    cells = cotangent_ref.shape[0]
    coeffs = basis_ref.shape[0]
    batches, batch_size = target_ref.shape
    small_copies = [
        pltpu.make_async_copy(src, dst, small_sems.at[k])
        for k, (src, dst) in enumerate(
            (
                (fill_hbm, fill_ref),
                (target_hbm, target_ref),
                (source_hbm, source_ref),
                (class_hbm, class_ref),
                (count_hbm, count_ref),
                (fetch_hbm, fetch_ref),
            )
        )
    ]
    remote = back_ref.shape[0]
    parts = 4
    step = cells // parts
    span = coeffs // parts
    basis_copy = Split(basis_hbm, basis_ref, sems.at[parts], 9)
    basis_copy.start()
    for copy in small_copies:
        copy.start()

    def cotangent_copy(part):
        rows = pl.ds(part * step, step)
        return pltpu.make_async_copy(cotangent_hbm.at[rows], cotangent_ref.at[rows], sems.at[part])

    def ops_copy(part):
        rows = pl.ds(part * span, span)
        return pltpu.make_async_copy(ops_hbm.at[rows], ops_ref.at[rows], ops_sems.at[part])

    for part in range(parts):
        cotangent_copy(part).start()
        ops_copy(part).start()
    rows = pl.ds(parts * span, coeffs - parts * span)
    rest_copy = pltpu.make_async_copy(ops_hbm.at[rows], ops_ref.at[rows], ops_sems.at[parts])
    rest_copy.start()
    clear(total_ref, remote)
    for copy in small_copies:
        copy.wait()

    batch = lax.broadcasted_iota(I32, (batches, batch_size), 0)
    slot = lax.broadcasted_iota(I32, (batches, batch_size), 1)
    fill = jnp.zeros((batches, batch_size), I32)
    for b in range(batches):
        fill = jnp.where(batch == b, fill_ref[b], fill)
    entry = source_ref[...] - cells
    far = (slot < fill) & (entry >= 0)
    found_ref[...] = jnp.where(far, encode(batch, entry, target_ref[...]), -1)
    code_copy = pltpu.make_async_copy(found_ref, code_ref, sems.at[parts + 1])
    code_copy.start()
    choose = choose_operators(class_ref, ops_ref, rows_ref)
    basis_copy.wait()
    spread_basis(basis_ref, wide_ref)
    code_copy.wait()

    share = cells // batches
    slots = batch_size // share
    dummy = encode(0, remote, 0)
    group = batches // parts

    def moments(part, place):
        cotangent_copy(part).wait()
        ops_copy(part).wait()
        for b in range(group):
            for k in range(b * span // group, (b + 1) * span // group):
                choose(part * span + k, 0)
            for q in range(share):
                i = (part * group + b) * share + q
                tile = masked_basis(wide_ref, count_ref, i).astype(BF)
                grad_ref[i] = dot(tile, cotangent_ref[i]).astype(BF)
                for p in range(q * slots, (q + 1) * slots):
                    code = code_ref[part * group + b, p]
                    list_ref[place] = code
                    place += 1 + (code >> 31)
            list_ref[place] = dummy
            place = ((place + 1) >> 1) << 1
        return place

    place = lax.fori_loop(0, parts, moments, 0)
    for q in range(2 * UNROLL):
        list_ref[place + q] = dummy
    turns = (place + 2 * UNROLL - 1) // (2 * UNROLL)
    rest_copy.wait()
    for k in range(parts * span, coeffs):
        choose(k, 0)

    def prepare(b, carry):
        wide = rows_ref[pl.ds(b, ROWS, stride=batches), :]
        op_ref[b] = wide.astype(BF)
        back_op_ref[b] = jnp.pad(wide, ((0, 128 - ROWS), (0, 0))).T[:ROWS].astype(BF)
        return carry

    lax.fori_loop(0, batches, prepare, 0, unroll=4)
    op_copy = pltpu.make_async_copy(op_ref, op_hbm, sems.at[parts])
    op_copy.start()

    def turn(j, carry):
        for q in range(UNROLL):
            d = 2 * (j * UNROLL + q)
            b, e0, t0 = decode(list_ref[d])
            _, e1, t1 = decode(list_ref[d + 1])
            result = dot(back_op_ref[b][:, :ROWS], jnp.concatenate([grad_ref[t0], grad_ref[t1]], axis=1))
            total_ref[e0] += result[:, :128]
            total_ref[e1] += result[:, 128:]
        return carry

    lax.fori_loop(0, turns, turn, 0)
    row = lax.broadcasted_iota(I32, (ROWS - MAIN, 128), 0)
    packed = flat(back_ref)

    def narrow(s, carry):
        tail = jnp.where(row == 1, fetch_ref[0, s].astype(F32), total_ref[s, MAIN:, :])
        tile = jnp.concatenate([total_ref[s, :MAIN, :], tail], axis=0).astype(BF)
        packed[block(s), :] = tile[:KEEP]
        return carry

    pieces = 8
    width = remote // pieces

    def send(part):
        rows = pl.ds(part * width, width)
        return pltpu.make_async_copy(back_ref.at[rows], back_hbm.at[rows], out_sems.at[part])

    def ship(part, carry):
        for q in range(width):
            narrow(part * width + q, 0)
        send(part).start()
        return carry

    lax.fori_loop(0, pieces, ship, 0)
    op_copy.wait()
    for part in range(pieces):
        send(part).wait()


def beside_kernel(
    count_ref,
    target_ref,
    source_ref,
    fill_ref,
    charges_hbm,
    cotangent_hbm,
    basis_hbm,
    op_ref,
    mult_hbm,
    local_ref,
    own_ref,
    atoms_ref,
    list_ref,
    charges_ref,
    cotangent_ref,
    basis_ref,
    wide_ref,
    mult_ref,
    packed_ref,
    grad_ref,
    back_op_ref,
    own_target,
    own_source,
    sems,
):
    cells = mult_ref.shape[0]
    batches = op_ref.shape[0]
    copies = [
        pltpu.make_async_copy(src, dst, sems.at[k])
        for k, (src, dst) in enumerate(
            ((basis_hbm, basis_ref), (charges_hbm, charges_ref), (cotangent_hbm, cotangent_ref))
        )
    ]
    for copy in copies:
        copy.start()
    clear(local_ref, cells)
    clear(own_ref, cells)
    for copy in copies:
        copy.wait()
    spread_basis(basis_ref, wide_ref)
    packed = flat(packed_ref)

    def turn(i, carry):
        tile = masked_basis(wide_ref, count_ref, i)
        both = jnp.concatenate([charges_ref[i], cotangent_ref[i]], axis=1)
        result = dot(tile.astype(BF), both).astype(BF)
        mult_ref[i] = result[:, :128]
        packed[block(i), :] = result[:KEEP, :128]
        grad_ref[i] = result[:, 128:]
        atoms_ref[i] = jnp.pad(tile, ((0, 128 - ROWS), (0, 0))).T.astype(BF)
        return carry

    lax.fori_loop(0, cells, turn, 0, unroll=4)
    mult_copy = pltpu.make_async_copy(packed_ref, mult_hbm, sems.at[0])
    mult_copy.start()

    def prepare(b, carry):
        wide = jnp.pad(op_ref[b].astype(F32), ((0, 128 - ROWS), (0, 0)))
        back_op_ref[b] = wide.T[:ROWS].astype(BF)
        return carry

    lax.fori_loop(0, batches, prepare, 0, unroll=2)
    dummy = encode(0, 0, cells)

    def batch(b, place):
        fill = fill_ref[b]

        def sort(p, places):
            own, far = places
            entry = source_ref[b, p] - cells
            target = target_ref[b, p]
            is_far = entry >= 0

            @pl.when(is_far)
            def _():
                list_ref[far] = encode(b, entry, target)

            @pl.when(jnp.logical_not(is_far))
            def _():
                own_target[own] = target
                own_source[own] = entry + cells

            step = is_far.astype(I32)
            return own + 1 - step, far + step

        own, far = lax.fori_loop(0, fill, sort, (0, place))
        list_ref[far] = dummy
        for q in range(8):
            own_target[own + q] = cells
            own_source[own + q] = cells
        op = op_ref[b][:, :ROWS]
        back_op = back_op_ref[b][:, :ROWS]

        def chunk(j, carry):
            for q in range(0, 8, 2):
                t0, t1 = own_target[j * 8 + q], own_target[j * 8 + q + 1]
                e0, e1 = own_source[j * 8 + q], own_source[j * 8 + q + 1]
                result = dot(op, jnp.concatenate([mult_ref[jnp.minimum(e0, cells - 1)], mult_ref[jnp.minimum(e1, cells - 1)]], axis=1))
                local_ref[t0] += result[:, :128]
                local_ref[t1] += result[:, 128:]
                result = dot(back_op, jnp.concatenate([grad_ref[jnp.minimum(t0, cells - 1)], grad_ref[jnp.minimum(t1, cells - 1)]], axis=1))
                own_ref[e0] += result[:, :128]
                own_ref[e1] += result[:, 128:]
            return carry

        lax.fori_loop(0, (own + 7) // 8, chunk, 0)
        return ((far + 1) // 2) * 2

    place = lax.fori_loop(0, batches, batch, 2)
    for q in range(2 * UNROLL):
        list_ref[place + q] = dummy
    list_ref[0] = (place - 2 + 2 * UNROLL - 1) // (2 * UNROLL)
    list_ref[1] = 0
    mult_copy.wait()


def pack_kernel(mult_hbm, back_hbm, out_hbm, asked_ref, mult_ref, tail_ref, wish_ref, sems):
    remote = back_hbm.shape[0]
    tail_copy = pltpu.make_async_copy(back_hbm.at[:, pl.ds(MAIN // 2, 1)], tail_ref, sems.at[0])
    tail_copy.start()
    mult_copy = Split(mult_hbm, mult_ref, sems.at[1], 8)
    mult_copy.start()
    row = lax.broadcasted_iota(I32, (16, 128), 0)
    lane = lax.broadcasted_iota(I32, (16, 128), 1)
    tails = tail_ref.reshape(2 * remote, 128)
    tail_copy.wait()
    wish = jnp.zeros((16, 128), F32)
    for g in range(remote // 8):
        tile = tails[16 * g : 16 * g + 16, :].astype(F32)
        wish = jnp.where(row == 2 * (lane - 8 * g) + 1, tile, wish)
    wish_ref[...] = jnp.sum(wish, axis=0, keepdims=True).astype(I32)
    wish_copy = pltpu.make_async_copy(wish_ref, asked_ref, sems.at[2])
    wish_copy.start()
    mult_copy.wait()
    wish_copy.wait()

    def one(s, carry):
        pltpu.make_async_copy(mult_ref.at[asked_ref[0, s]], out_hbm.at[s], sems.at[3]).start()
        return carry

    lax.fori_loop(0, remote, one, 0, unroll=8)
    pltpu.make_async_copy(back_hbm, out_hbm, sems.at[3]).wait()


def charge_kernel(asked_ref, returned_hbm, own_hbm, atoms_hbm, charge_hbm, returned_ref, own_ref, atoms_ref, charge_ref, sems):
    cells = charge_ref.shape[0]
    remote = returned_ref.shape[0]
    copies = [
        pltpu.make_async_copy(src, dst, sems.at[k])
        for k, (src, dst) in enumerate(((own_hbm, own_ref), (returned_hbm, returned_ref), (atoms_hbm, atoms_ref)))
    ]
    for copy in copies:
        copy.start()
    for copy in copies:
        copy.wait()
    packed = flat(returned_ref)

    def collect(s, carry):
        own_ref[asked_ref[0, s], :KEEP, :] += packed[block(s), :].astype(F32)
        return carry

    lax.fori_loop(0, remote, collect, 0, unroll=4)
    row = lax.broadcasted_iota(I32, (ROWS, 128), 0)

    def atoms(i, carry):
        grads = jnp.where(row > MAIN, 0.0, own_ref[i]).astype(BF)
        charge_ref[i] = dot(atoms_ref[i][:, :ROWS], grads).astype(BF)
        return carry

    lax.fori_loop(0, cells, atoms, 0, unroll=4)
    out = pltpu.make_async_copy(charge_ref, charge_hbm, sems.at[0])
    out.start()
    out.wait()


def far_kernel(
    list_hbm,
    incoming_ref,
    local_hbm,
    atoms_hbm,
    op_hbm,
    potential_hbm,
    list_ref,
    local_ref,
    atoms_ref,
    op_ref,
    sum_ref,
    potential_ref,
    sems,
    out_sems,
):
    cells = atoms_ref.shape[0]
    copies = [
        Split(src, dst, sems.at[k], pieces)
        for k, (src, dst, pieces) in enumerate(
            (
                (list_hbm, list_ref, 1),
                (op_hbm, op_ref, 2),
                (atoms_hbm, atoms_ref, 4),
                (local_hbm, local_ref, 5),
            )
        )
    ]
    for copy in copies:
        copy.start()
    clear(sum_ref, cells)
    packed = flat(incoming_ref)
    for copy in copies[:2]:
        copy.wait()

    def turn(j, carry):
        for q in range(UNROLL):
            d = 2 * (j * UNROLL + q + 1)
            b, e0, t0 = decode(list_ref[d])
            _, e1, t1 = decode(list_ref[d + 1])
            both = jnp.concatenate([packed[block(e0), :], packed[block(e1), :]], axis=1)
            result = dot(op_ref[b][:, :KEEP], both)
            sum_ref[t0] += result[:, :128]
            sum_ref[t1] += result[:, 128:]
        return carry

    lax.fori_loop(0, list_ref[0], turn, 0)
    for copy in copies[2:]:
        copy.wait()

    def atoms(i, carry):
        whole = (sum_ref[i] + local_ref[i]).astype(BF)
        potential_ref[i] = dot(atoms_ref[i][:, :ROWS], whole).astype(BF)
        return carry

    outs = []
    parts = 8
    width = cells // parts
    for part in range(parts):
        lax.fori_loop(part * width, (part + 1) * width, atoms, 0, unroll=8)
        rows = pl.ds(part * width, width)
        copy = pltpu.make_async_copy(potential_ref.at[rows], potential_hbm.at[rows], out_sems.at[part])
        copy.start()
        outs.append(copy)
    for copy in outs:
        copy.wait()


SMEM = pl.BlockSpec(memory_space=pltpu.SMEM)
VMEM = pl.BlockSpec(memory_space=pltpu.VMEM)
ANY = pl.BlockSpec(memory_space=pl.ANY)
Shape = jax.ShapeDtypeStruct


def call_back(leaf_count, fill, wishes, batch_class, targets, sources, cotangent, basis_major, ops_major):
    coeffs, cells, slots = basis_major.shape
    domains = wishes.shape[1]
    batches, batch_size = targets.shape
    channels = cotangent.shape[2]
    return pl.pallas_call(
        back_kernel,
        out_shape=(
            Shape((domains, KEEP // 2, 2, channels), BF),
            Shape((batches, ROWS, 128), BF),
        ),
        in_specs=[ANY] * 9,
        out_specs=(ANY, ANY),
        scratch_shapes=[
            pltpu.SMEM(leaf_count.shape, I32),
            pltpu.SMEM(fill.shape, I32),
            pltpu.SMEM(wishes.shape, I32),
            pltpu.SMEM(batch_class.shape, I32),
            pltpu.VMEM(targets.shape, I32),
            pltpu.VMEM(sources.shape, I32),
            pltpu.VMEM((cells, slots, channels), BF),
            pltpu.VMEM((coeffs, cells, slots), BF),
            pltpu.VMEM(ops_major.shape, BF),
            pltpu.VMEM((ROWS * STRIDE, slots), F32),
            pltpu.VMEM((ROWS * batches, 128), F32),
            pltpu.VMEM((cells, ROWS, channels), BF),
            pltpu.VMEM((domains + 1, ROWS, channels), F32),
            pltpu.VMEM((domains, KEEP // 2, 2, channels), BF),
            pltpu.VMEM((batches, ROWS, 128), BF),
            pltpu.VMEM((batches, ROWS, 128), BF),
            pltpu.VMEM((batches, batch_size), I32),
            pltpu.SMEM((batches, batch_size), I32),
            pltpu.SMEM((batches * batch_size + 2 * UNROLL + 2,), I32),
            pltpu.SemaphoreType.DMA((6,)),
            pltpu.SemaphoreType.DMA((6,)),
            pltpu.SemaphoreType.DMA((5,)),
            pltpu.SemaphoreType.DMA((8,)),
        ],
        compiler_params=params(),
        name="back_pairs",
    )(leaf_count, fill, wishes, batch_class, targets, sources, cotangent, basis_major, ops_major)


def call_beside(leaf_count, targets, sources, fill, charges, cotangent, basis_major, ops):
    coeffs, cells, slots = basis_major.shape
    batches, batch_size = targets.shape
    channels = charges.shape[2]
    return pl.pallas_call(
        beside_kernel,
        out_shape=(
            Shape((cells, KEEP // 2, 2, channels), BF),
            Shape((cells + 1, ROWS, channels), F32),
            Shape((cells + 1, ROWS, channels), F32),
            Shape((cells, slots, 128), BF),
            Shape((batches * batch_size + 2 * UNROLL + 4,), I32),
        ),
        in_specs=[SMEM] * 4 + [ANY] * 3 + [VMEM],
        out_specs=(ANY, VMEM, VMEM, VMEM, SMEM),
        scratch_shapes=[
            pltpu.VMEM((cells, slots, channels), BF),
            pltpu.VMEM((cells, slots, channels), BF),
            pltpu.VMEM((coeffs, cells, slots), BF),
            pltpu.VMEM((ROWS * STRIDE, slots), F32),
            pltpu.VMEM((cells, ROWS, channels), BF),
            pltpu.VMEM((cells, KEEP // 2, 2, channels), BF),
            pltpu.VMEM((cells, ROWS, channels), BF),
            pltpu.VMEM((batches, ROWS, 128), BF),
            pltpu.SMEM((batch_size + 8,), I32),
            pltpu.SMEM((batch_size + 8,), I32),
            pltpu.SemaphoreType.DMA((3,)),
        ],
        compiler_params=params(),
        cost_estimate=pl.CostEstimate(flops=400_000_000, bytes_accessed=8_000_000, transcendentals=0),
        name="own_pairs",
    )(leaf_count, targets, sources, fill, charges, cotangent, basis_major, ops)


def call_pack(mult, returned):
    cells, _, _, channels = mult.shape
    domains = returned.shape[0]
    return pl.pallas_call(
        pack_kernel,
        out_shape=(Shape(returned.shape, BF), Shape((1, domains), I32)),
        in_specs=[ANY] * 2,
        out_specs=(ANY, SMEM),
        scratch_shapes=[
            pltpu.VMEM(mult.shape, BF),
            pltpu.VMEM((domains, 1, 2, channels), BF),
            pltpu.VMEM((1, domains), I32),
            pltpu.SemaphoreType.DMA((4,)),
        ],
        compiler_params=params(),
        name="pack_blocks",
    )(mult, returned)


def call_charge(asked, returned, own, atoms):
    cells, slots, _ = atoms.shape
    channels = returned.shape[3]
    return pl.pallas_call(
        charge_kernel,
        out_shape=Shape((cells, slots, channels), BF),
        in_specs=[SMEM] + [ANY] * 3,
        out_specs=ANY,
        scratch_shapes=[
            pltpu.VMEM(returned.shape, BF),
            pltpu.VMEM(own.shape, F32),
            pltpu.VMEM((cells, slots, 128), BF),
            pltpu.VMEM((cells, slots, channels), BF),
            pltpu.SemaphoreType.DMA((3,)),
        ],
        compiler_params=params(52),
        cost_estimate=pl.CostEstimate(flops=200_000_000, bytes_accessed=8_000_000, transcendentals=0),
        name="charge_atoms",
    )(asked, returned, own, atoms)


def call_far(pairs, incoming, local_part, atoms, ops):
    cells, slots, _ = atoms.shape
    channels = incoming.shape[3]
    return pl.pallas_call(
        far_kernel,
        out_shape=Shape((cells, slots, channels), BF),
        in_specs=[ANY, VMEM] + [ANY] * 3,
        out_specs=ANY,
        scratch_shapes=[
            pltpu.SMEM(pairs.shape, I32),
            pltpu.VMEM(local_part.shape, F32),
            pltpu.VMEM((cells, slots, 128), BF),
            pltpu.VMEM(ops.shape, BF),
            pltpu.VMEM((cells + 1, ROWS, channels), F32),
            pltpu.VMEM((cells, slots, channels), BF),
            pltpu.SemaphoreType.DMA((5,)),
            pltpu.SemaphoreType.DMA((8,)),
        ],
        compiler_params=params(49),
        name="far_pairs_atoms",
    )(pairs, incoming, local_part, atoms, ops)


def local(
    charges,
    basis,
    leaf_count,
    cotangent,
    m2l_ops,
    fetch_cells,
    pair_target,
    pair_source,
    batch_class,
    batch_fill,
):
    basis_major = basis.transpose(1, 0, 2)
    wishes = fetch_cells.reshape(1, -1)
    targets, sources, fill = pair_target[0], pair_source[0], batch_fill[0]
    back, ops = call_back(
        leaf_count, fill, wishes, batch_class[0], targets, sources, cotangent, basis_major, m2l_ops.transpose(1, 2, 0)
    )
    returned = lax.all_to_all(back, ("dx", "dy"), split_axis=0, concat_axis=0, tiled=True)
    mult, local_part, own, atoms, pairs = call_beside(
        leaf_count, targets, sources, fill, charges, cotangent, basis_major, ops
    )
    outgoing, asked = call_pack(mult, returned)
    incoming = lax.all_to_all(outgoing, ("dx", "dy"), split_axis=0, concat_axis=0, tiled=True)
    charge_grad = call_charge(asked, returned, own, atoms)
    potential = call_far(pairs, incoming, local_part, atoms, ops)
    return potential, charge_grad


def solution(mesh):
    in_specs = (
        P(("dx", "dy"), None, None),
        P(("dx", "dy"), None, None),
        P(("dx", "dy")),
        P(("dx", "dy"), None, None),
        P(),
        P(("dx", "dy"), None, None),
        P(("dx", "dy"), None, None),
        P(("dx", "dy"), None, None),
        P(("dx", "dy"), None),
        P(("dx", "dy"), None),
    )
    out_specs = (P(("dx", "dy"), None, None), P(("dx", "dy"), None, None))
    return jax.shard_map(local, mesh=mesh, in_specs=in_specs, out_specs=out_specs, check_vma=False)
```

```python
import jax
import jax.numpy as jnp
from jax import lax
from jax.experimental import pallas as pl
from jax.experimental.pallas import tpu as pltpu
from jax.sharding import PartitionSpec as P

BF = jnp.bfloat16
F32 = jnp.float32
I32 = jnp.int32
ROWS = 88
MAIN = 80
KEEP = 82
STRIDE = 72
UNROLL = 16
LIMIT = 62


def dot(a, b):
    return lax.dot_general(a, b, (((1,), (0,)), ((), ())), preferred_element_type=F32)


def params(mib=LIMIT):
    return pltpu.CompilerParams(vmem_limit_bytes=mib << 20)


def flat(ref):
    return ref.reshape(ref.shape[0] * KEEP, ref.shape[-1])


def block(index):
    return pl.ds(pl.multiple_of(index * KEEP, 2), KEEP)


def spread_basis(basis_ref, wide_ref):
    coeffs, cells, slots = basis_ref.shape

    def put(k, carry):
        wide_ref[pl.ds(pl.multiple_of(k * STRIDE, 8), cells), :] = basis_ref[k].astype(F32)
        return carry

    lax.fori_loop(0, coeffs, put, 0, unroll=9)
    wide_ref[coeffs * STRIDE :, :] = jnp.zeros(((ROWS - coeffs) * STRIDE, slots), F32)


def masked_basis(wide_ref, count_ref, cell):
    tile = wide_ref[pl.ds(cell, ROWS, stride=STRIDE), :]
    lane = lax.broadcasted_iota(I32, tile.shape, 1)
    return jnp.where(lane < count_ref[cell], tile, 0.0)


class Split:
    def __init__(self, src, dst, sem, pieces):
        self.src, self.dst, self.sem, self.pieces = src, dst, sem, pieces

    def start(self):
        size = self.src.shape[0]
        edges = [size * k // self.pieces for k in range(self.pieces + 1)]
        for low, high in zip(edges, edges[1:]):
            rows = pl.ds(low, high - low)
            pltpu.make_async_copy(self.src.at[rows], self.dst.at[rows], self.sem).start()

    def wait(self):
        pltpu.make_async_copy(self.src, self.dst, self.sem).wait()


def clear(ref, count):
    def one(e, carry):
        ref[e] = jnp.zeros(ref.shape[1:], ref.dtype)
        return carry

    lax.fori_loop(0, count, one, 0, unroll=8)


def encode(batch, entry, target):
    return batch * 65536 + entry * 256 + target


def decode(code):
    return code >> 16, (code >> 8) & 255, code & 255


def choose_operators(class_ref, ops_ref, rows_ref):
    coeffs, _, classes = ops_ref.shape
    batches = rows_ref.shape[0] // ROWS
    rows_ref[...] = jnp.zeros(rows_ref.shape, F32)
    row = lax.broadcasted_iota(I32, (batches, classes), 0)
    wanted = jnp.zeros((batches, classes), I32)
    for b in range(batches):
        wanted = jnp.where(row == b, class_ref[b], wanted)
    hot = (wanted == lax.broadcasted_iota(I32, (batches, classes), 1)).astype(F32).astype(BF)

    def one(k, carry):
        picked = lax.dot_general(hot, ops_ref[k], (((1,), (1,)), ((), ())), preferred_element_type=F32)
        rows_ref[pl.ds(pl.multiple_of(k * batches, batches), batches), :coeffs] = picked
        return carry

    return one


def back_kernel(
    count_hbm,
    fill_hbm,
    fetch_hbm,
    class_hbm,
    target_hbm,
    source_hbm,
    cotangent_hbm,
    basis_hbm,
    ops_hbm,
    back_hbm,
    op_hbm,
    count_ref,
    fill_ref,
    fetch_ref,
    class_ref,
    target_ref,
    source_ref,
    cotangent_ref,
    basis_ref,
    ops_ref,
    wide_ref,
    rows_ref,
    grad_ref,
    total_ref,
    back_ref,
    op_ref,
    back_op_ref,
    found_ref,
    code_ref,
    list_ref,
    small_sems,
    sems,
    ops_sems,
    out_sems,
):
    cells = cotangent_ref.shape[0]
    coeffs = basis_ref.shape[0]
    batches, batch_size = target_ref.shape
    small_copies = [
        pltpu.make_async_copy(src, dst, small_sems.at[k])
        for k, (src, dst) in enumerate(
            (
                (fill_hbm, fill_ref),
                (target_hbm, target_ref),
                (source_hbm, source_ref),
                (class_hbm, class_ref),
                (count_hbm, count_ref),
                (fetch_hbm, fetch_ref),
            )
        )
    ]
    remote = back_ref.shape[0]
    parts = 4
    step = cells // parts
    span = coeffs // parts
    basis_copy = Split(basis_hbm, basis_ref, sems.at[parts], 9)
    basis_copy.start()
    for copy in small_copies:
        copy.start()

    def cotangent_copy(part):
        rows = pl.ds(part * step, step)
        return pltpu.make_async_copy(cotangent_hbm.at[rows], cotangent_ref.at[rows], sems.at[part])

    def ops_copy(part):
        rows = pl.ds(part * span, span)
        return pltpu.make_async_copy(ops_hbm.at[rows], ops_ref.at[rows], ops_sems.at[part])

    for part in range(parts):
        cotangent_copy(part).start()
        ops_copy(part).start()
    rows = pl.ds(parts * span, coeffs - parts * span)
    rest_copy = pltpu.make_async_copy(ops_hbm.at[rows], ops_ref.at[rows], ops_sems.at[parts])
    rest_copy.start()
    clear(total_ref, remote)
    for copy in small_copies:
        copy.wait()

    batch = lax.broadcasted_iota(I32, (batches, batch_size), 0)
    slot = lax.broadcasted_iota(I32, (batches, batch_size), 1)
    fill = jnp.zeros((batches, batch_size), I32)
    for b in range(batches):
        fill = jnp.where(batch == b, fill_ref[b], fill)
    entry = source_ref[...] - cells
    far = (slot < fill) & (entry >= 0)
    found_ref[...] = jnp.where(far, encode(batch, entry, target_ref[...]), -1)
    code_copy = pltpu.make_async_copy(found_ref, code_ref, sems.at[parts + 1])
    code_copy.start()
    choose = choose_operators(class_ref, ops_ref, rows_ref)
    basis_copy.wait()
    spread_basis(basis_ref, wide_ref)
    code_copy.wait()

    share = cells // batches
    slots = batch_size // share
    dummy = encode(0, remote, 0)
    group = batches // parts

    def moments(part, place):
        cotangent_copy(part).wait()
        ops_copy(part).wait()
        for b in range(group):
            for k in range(b * span // group, (b + 1) * span // group):
                choose(part * span + k, 0)
            for q in range(share):
                i = (part * group + b) * share + q
                tile = masked_basis(wide_ref, count_ref, i).astype(BF)
                grad_ref[i] = dot(tile, cotangent_ref[i]).astype(BF)
                for p in range(q * slots, (q + 1) * slots):
                    code = code_ref[part * group + b, p]
                    list_ref[place] = code
                    place += 1 + (code >> 31)
            list_ref[place] = dummy
            place = ((place + 1) >> 1) << 1
        return place

    place = lax.fori_loop(0, parts, moments, 0)
    for q in range(2 * UNROLL):
        list_ref[place + q] = dummy
    turns = (place + 2 * UNROLL - 1) // (2 * UNROLL)
    rest_copy.wait()
    for k in range(parts * span, coeffs):
        choose(k, 0)

    def prepare(b, carry):
        wide = rows_ref[pl.ds(b, ROWS, stride=batches), :]
        op_ref[b] = wide.astype(BF)
        back_op_ref[b] = jnp.pad(wide, ((0, 128 - ROWS), (0, 0))).T[:ROWS].astype(BF)
        return carry

    lax.fori_loop(0, batches, prepare, 0, unroll=4)
    op_copy = pltpu.make_async_copy(op_ref, op_hbm, sems.at[parts])
    op_copy.start()

    def turn(j, carry):
        for q in range(UNROLL):
            d = 2 * (j * UNROLL + q)
            b, e0, t0 = decode(list_ref[d])
            _, e1, t1 = decode(list_ref[d + 1])
            result = dot(back_op_ref[b][:, :ROWS], jnp.concatenate([grad_ref[t0], grad_ref[t1]], axis=1))
            total_ref[e0] += result[:, :128]
            total_ref[e1] += result[:, 128:]
        return carry

    lax.fori_loop(0, turns, turn, 0)
    row = lax.broadcasted_iota(I32, (ROWS - MAIN, 128), 0)
    packed = flat(back_ref)

    def narrow(s, carry):
        tail = jnp.where(row == 1, fetch_ref[0, s].astype(F32), total_ref[s, MAIN:, :])
        tile = jnp.concatenate([total_ref[s, :MAIN, :], tail], axis=0).astype(BF)
        packed[block(s), :] = tile[:KEEP]
        return carry

    pieces = 8
    width = remote // pieces

    def send(part):
        rows = pl.ds(part * width, width)
        return pltpu.make_async_copy(back_ref.at[rows], back_hbm.at[rows], out_sems.at[part])

    def ship(part, carry):
        for q in range(width):
            narrow(part * width + q, 0)
        send(part).start()
        return carry

    lax.fori_loop(0, pieces, ship, 0)
    op_copy.wait()
    for part in range(pieces):
        send(part).wait()


def beside_kernel(
    count_ref,
    target_ref,
    source_ref,
    fill_ref,
    charges_hbm,
    cotangent_hbm,
    basis_hbm,
    op_ref,
    mult_hbm,
    local_ref,
    own_ref,
    atoms_ref,
    list_ref,
    charges_ref,
    cotangent_ref,
    basis_ref,
    wide_ref,
    mult_ref,
    packed_ref,
    grad_ref,
    back_op_ref,
    own_target,
    own_source,
    sems,
):
    cells = mult_ref.shape[0]
    batches = op_ref.shape[0]
    copies = [
        pltpu.make_async_copy(src, dst, sems.at[k])
        for k, (src, dst) in enumerate(
            ((basis_hbm, basis_ref), (charges_hbm, charges_ref), (cotangent_hbm, cotangent_ref))
        )
    ]
    for copy in copies:
        copy.start()
    clear(local_ref, cells)
    clear(own_ref, cells)
    for copy in copies:
        copy.wait()
    spread_basis(basis_ref, wide_ref)
    packed = flat(packed_ref)

    def turn(i, carry):
        tile = masked_basis(wide_ref, count_ref, i)
        both = jnp.concatenate([charges_ref[i], cotangent_ref[i]], axis=1)
        result = dot(tile.astype(BF), both).astype(BF)
        mult_ref[i] = result[:, :128]
        packed[block(i), :] = result[:KEEP, :128]
        grad_ref[i] = result[:, 128:]
        atoms_ref[i] = jnp.pad(tile, ((0, 128 - ROWS), (0, 0))).T.astype(BF)
        return carry

    lax.fori_loop(0, cells, turn, 0, unroll=4)
    mult_copy = pltpu.make_async_copy(packed_ref, mult_hbm, sems.at[0])
    mult_copy.start()

    def prepare(b, carry):
        wide = jnp.pad(op_ref[b].astype(F32), ((0, 128 - ROWS), (0, 0)))
        back_op_ref[b] = wide.T[:ROWS].astype(BF)
        return carry

    lax.fori_loop(0, batches, prepare, 0, unroll=2)
    dummy = encode(0, 0, cells)

    def batch(b, place):
        fill = fill_ref[b]

        def sort(p, places):
            own, far = places
            entry = source_ref[b, p] - cells
            target = target_ref[b, p]
            is_far = entry >= 0

            @pl.when(is_far)
            def _():
                list_ref[far] = encode(b, entry, target)

            @pl.when(jnp.logical_not(is_far))
            def _():
                own_target[own] = target
                own_source[own] = entry + cells

            step = is_far.astype(I32)
            return own + 1 - step, far + step

        own, far = lax.fori_loop(0, fill, sort, (0, place))
        list_ref[far] = dummy
        for q in range(8):
            own_target[own + q] = cells
            own_source[own + q] = cells
        op = op_ref[b][:, :ROWS]
        back_op = back_op_ref[b][:, :ROWS]

        def chunk(j, carry):
            for q in range(0, 8, 2):
                t0, t1 = own_target[j * 8 + q], own_target[j * 8 + q + 1]
                e0, e1 = own_source[j * 8 + q], own_source[j * 8 + q + 1]
                result = dot(op, jnp.concatenate([mult_ref[jnp.minimum(e0, cells - 1)], mult_ref[jnp.minimum(e1, cells - 1)]], axis=1))
                local_ref[t0] += result[:, :128]
                local_ref[t1] += result[:, 128:]
                result = dot(back_op, jnp.concatenate([grad_ref[jnp.minimum(t0, cells - 1)], grad_ref[jnp.minimum(t1, cells - 1)]], axis=1))
                own_ref[e0] += result[:, :128]
                own_ref[e1] += result[:, 128:]
            return carry

        lax.fori_loop(0, (own + 7) // 8, chunk, 0)
        return ((far + 1) // 2) * 2

    place = lax.fori_loop(0, batches, batch, 2)
    for q in range(2 * UNROLL):
        list_ref[place + q] = dummy
    list_ref[0] = (place - 2 + 2 * UNROLL - 1) // (2 * UNROLL)
    list_ref[1] = 0
    mult_copy.wait()


def pack_kernel(mult_hbm, back_hbm, out_hbm, asked_ref, mult_ref, tail_ref, wish_ref, sems):
    remote = back_hbm.shape[0]
    tail_copy = pltpu.make_async_copy(back_hbm.at[:, pl.ds(MAIN // 2, 1)], tail_ref, sems.at[0])
    tail_copy.start()
    mult_copy = Split(mult_hbm, mult_ref, sems.at[1], 8)
    mult_copy.start()
    row = lax.broadcasted_iota(I32, (16, 128), 0)
    lane = lax.broadcasted_iota(I32, (16, 128), 1)
    tails = tail_ref.reshape(2 * remote, 128)
    tail_copy.wait()
    wish = jnp.zeros((16, 128), F32)
    for g in range(remote // 8):
        tile = tails[16 * g : 16 * g + 16, :].astype(F32)
        wish = jnp.where(row == 2 * (lane - 8 * g) + 1, tile, wish)
    wish_ref[...] = jnp.sum(wish, axis=0, keepdims=True).astype(I32)
    wish_copy = pltpu.make_async_copy(wish_ref, asked_ref, sems.at[2])
    wish_copy.start()
    mult_copy.wait()
    wish_copy.wait()

    def one(s, carry):
        pltpu.make_async_copy(mult_ref.at[asked_ref[0, s]], out_hbm.at[s], sems.at[3]).start()
        return carry

    lax.fori_loop(0, remote, one, 0, unroll=8)
    pltpu.make_async_copy(back_hbm, out_hbm, sems.at[3]).wait()


def charge_kernel(asked_ref, returned_hbm, own_hbm, atoms_hbm, charge_hbm, returned_ref, own_ref, atoms_ref, charge_ref, sems):
    cells = charge_ref.shape[0]
    remote = returned_ref.shape[0]
    copies = [
        pltpu.make_async_copy(src, dst, sems.at[k])
        for k, (src, dst) in enumerate(((own_hbm, own_ref), (returned_hbm, returned_ref), (atoms_hbm.at[pl.ds(0, cells)], atoms_ref)))
    ]
    for copy in copies:
        copy.start()
    for copy in copies:
        copy.wait()
    packed = flat(returned_ref)

    def collect(s, carry):
        own_ref[asked_ref[0, s], :KEEP, :] += packed[block(s), :].astype(F32)
        return carry

    lax.fori_loop(0, remote, collect, 0, unroll=4)
    row = lax.broadcasted_iota(I32, (ROWS, 128), 0)

    def atoms(i, carry):
        grads = jnp.where(row > MAIN, 0.0, own_ref[i]).astype(BF)
        charge_ref[i] = dot(atoms_ref[i][:, :ROWS], grads).astype(BF)
        return carry

    lax.fori_loop(0, cells, atoms, 0, unroll=4)
    out = pltpu.make_async_copy(charge_ref, charge_hbm, sems.at[0])
    out.start()
    out.wait()


def far_kernel(
    list_hbm,
    incoming_ref,
    local_hbm,
    atoms_hbm,
    op_hbm,
    potential_hbm,
    list_ref,
    local_ref,
    atoms_ref,
    op_ref,
    sum_ref,
    potential_ref,
    sems,
    out_sems,
):
    cells = atoms_ref.shape[0]
    copies = [
        Split(src, dst, sems.at[k], pieces)
        for k, (src, dst, pieces) in enumerate(
            (
                (list_hbm, list_ref, 1),
                (op_hbm, op_ref, 2),
                (atoms_hbm.at[pl.ds(0, cells)], atoms_ref, 4),
                (local_hbm.at[pl.ds(0, cells)], local_ref, 4),
            )
        )
    ]
    for copy in copies:
        copy.start()
    clear(sum_ref, cells)
    packed = flat(incoming_ref)
    for copy in copies[:2]:
        copy.wait()

    def turn(j, carry):
        for q in range(UNROLL):
            d = 2 * (j * UNROLL + q + 1)
            b, e0, t0 = decode(list_ref[d])
            _, e1, t1 = decode(list_ref[d + 1])
            both = jnp.concatenate([packed[block(e0), :], packed[block(e1), :]], axis=1)
            result = dot(op_ref[b][:, :KEEP], both)
            sum_ref[t0] += result[:, :128]
            sum_ref[t1] += result[:, 128:]
        return carry

    lax.fori_loop(0, list_ref[0], turn, 0)
    for copy in copies[2:]:
        copy.wait()

    def atoms(i, carry):
        whole = (sum_ref[i] + local_ref[i]).astype(BF)
        potential_ref[i] = dot(atoms_ref[i][:, :ROWS], whole).astype(BF)
        return carry

    outs = []
    parts = 8
    width = cells // parts
    for part in range(parts):
        lax.fori_loop(part * width, (part + 1) * width, atoms, 0, unroll=8)
        rows = pl.ds(part * width, width)
        copy = pltpu.make_async_copy(potential_ref.at[rows], potential_hbm.at[rows], out_sems.at[part])
        copy.start()
        outs.append(copy)
    for copy in outs:
        copy.wait()


SMEM = pl.BlockSpec(memory_space=pltpu.SMEM)
VMEM = pl.BlockSpec(memory_space=pltpu.VMEM)
ANY = pl.BlockSpec(memory_space=pl.ANY)
Shape = jax.ShapeDtypeStruct


def call_back(leaf_count, fill, wishes, batch_class, targets, sources, cotangent, basis_major, ops_major):
    coeffs, cells, slots = basis_major.shape
    domains = wishes.shape[1]
    batches, batch_size = targets.shape
    channels = cotangent.shape[2]
    return pl.pallas_call(
        back_kernel,
        out_shape=(
            Shape((domains, KEEP // 2, 2, channels), BF),
            Shape((batches, ROWS, 128), BF),
        ),
        in_specs=[ANY] * 9,
        out_specs=(ANY, ANY),
        scratch_shapes=[
            pltpu.SMEM(leaf_count.shape, I32),
            pltpu.SMEM(fill.shape, I32),
            pltpu.SMEM(wishes.shape, I32),
            pltpu.SMEM(batch_class.shape, I32),
            pltpu.VMEM(targets.shape, I32),
            pltpu.VMEM(sources.shape, I32),
            pltpu.VMEM((cells, slots, channels), BF),
            pltpu.VMEM((coeffs, cells, slots), BF),
            pltpu.VMEM(ops_major.shape, BF),
            pltpu.VMEM((ROWS * STRIDE, slots), F32),
            pltpu.VMEM((ROWS * batches, 128), F32),
            pltpu.VMEM((cells, ROWS, channels), BF),
            pltpu.VMEM((domains + 1, ROWS, channels), F32),
            pltpu.VMEM((domains, KEEP // 2, 2, channels), BF),
            pltpu.VMEM((batches, ROWS, 128), BF),
            pltpu.VMEM((batches, ROWS, 128), BF),
            pltpu.VMEM((batches, batch_size), I32),
            pltpu.SMEM((batches, batch_size), I32),
            pltpu.SMEM((batches * batch_size + 2 * UNROLL + 2,), I32),
            pltpu.SemaphoreType.DMA((6,)),
            pltpu.SemaphoreType.DMA((6,)),
            pltpu.SemaphoreType.DMA((5,)),
            pltpu.SemaphoreType.DMA((8,)),
        ],
        compiler_params=params(),
        name="back_pairs",
    )(leaf_count, fill, wishes, batch_class, targets, sources, cotangent, basis_major, ops_major)


def call_beside(leaf_count, targets, sources, fill, charges, cotangent, basis_major, ops):
    coeffs, cells, slots = basis_major.shape
    batches, batch_size = targets.shape
    channels = charges.shape[2]
    return pl.pallas_call(
        beside_kernel,
        out_shape=(
            Shape((cells, KEEP // 2, 2, channels), BF),
            Shape((2 * cells, ROWS, channels), F32),
            Shape((cells + 1, ROWS, channels), F32),
            Shape((2 * cells, slots, 128), BF),
            Shape((batches * batch_size + 2 * UNROLL + 4,), I32),
        ),
        in_specs=[SMEM] * 4 + [ANY] * 3 + [VMEM],
        out_specs=(ANY, VMEM, VMEM, VMEM, SMEM),
        scratch_shapes=[
            pltpu.VMEM((cells, slots, channels), BF),
            pltpu.VMEM((cells, slots, channels), BF),
            pltpu.VMEM((coeffs, cells, slots), BF),
            pltpu.VMEM((ROWS * STRIDE, slots), F32),
            pltpu.VMEM((cells, ROWS, channels), BF),
            pltpu.VMEM((cells, KEEP // 2, 2, channels), BF),
            pltpu.VMEM((cells, ROWS, channels), BF),
            pltpu.VMEM((batches, ROWS, 128), BF),
            pltpu.SMEM((batch_size + 8,), I32),
            pltpu.SMEM((batch_size + 8,), I32),
            pltpu.SemaphoreType.DMA((3,)),
        ],
        compiler_params=params(),
        cost_estimate=pl.CostEstimate(flops=400_000_000, bytes_accessed=8_000_000, transcendentals=0),
        name="own_pairs",
    )(leaf_count, targets, sources, fill, charges, cotangent, basis_major, ops)


def call_pack(mult, returned):
    cells, _, _, channels = mult.shape
    domains = returned.shape[0]
    return pl.pallas_call(
        pack_kernel,
        out_shape=(Shape(returned.shape, BF), Shape((1, domains), I32)),
        in_specs=[ANY] * 2,
        out_specs=(ANY, SMEM),
        scratch_shapes=[
            pltpu.VMEM(mult.shape, BF),
            pltpu.VMEM((domains, 1, 2, channels), BF),
            pltpu.VMEM((1, domains), I32),
            pltpu.SemaphoreType.DMA((4,)),
        ],
        compiler_params=params(),
        name="pack_blocks",
    )(mult, returned)


def call_charge(asked, returned, own, atoms):
    cells, slots = own.shape[0] - 1, atoms.shape[1]
    channels = returned.shape[3]
    return pl.pallas_call(
        charge_kernel,
        out_shape=Shape((cells, slots, channels), BF),
        in_specs=[SMEM] + [ANY] * 3,
        out_specs=ANY,
        scratch_shapes=[
            pltpu.VMEM(returned.shape, BF),
            pltpu.VMEM(own.shape, F32),
            pltpu.VMEM((cells, slots, 128), BF),
            pltpu.VMEM((cells, slots, channels), BF),
            pltpu.SemaphoreType.DMA((3,)),
        ],
        compiler_params=params(52),
        cost_estimate=pl.CostEstimate(flops=200_000_000, bytes_accessed=8_000_000, transcendentals=0),
        name="charge_atoms",
    )(asked, returned, own, atoms)


def call_far(pairs, incoming, local_part, atoms, ops):
    cells, slots = atoms.shape[0] // 2, atoms.shape[1]
    channels = incoming.shape[3]
    return pl.pallas_call(
        far_kernel,
        out_shape=Shape((cells, slots, channels), BF),
        in_specs=[ANY, VMEM] + [ANY] * 3,
        out_specs=ANY,
        scratch_shapes=[
            pltpu.SMEM(pairs.shape, I32),
            pltpu.VMEM((cells, ROWS, channels), F32),
            pltpu.VMEM((cells, slots, 128), BF),
            pltpu.VMEM(ops.shape, BF),
            pltpu.VMEM((cells + 1, ROWS, channels), F32),
            pltpu.VMEM((cells, slots, channels), BF),
            pltpu.SemaphoreType.DMA((5,)),
            pltpu.SemaphoreType.DMA((8,)),
        ],
        compiler_params=params(49),
        name="far_pairs_atoms",
    )(pairs, incoming, local_part, atoms, ops)


def local(
    charges,
    basis,
    leaf_count,
    cotangent,
    m2l_ops,
    fetch_cells,
    pair_target,
    pair_source,
    batch_class,
    batch_fill,
):
    basis_major = basis.transpose(1, 0, 2)
    wishes = fetch_cells.reshape(1, -1)
    targets, sources, fill = pair_target[0], pair_source[0], batch_fill[0]
    back, ops = call_back(
        leaf_count, fill, wishes, batch_class[0], targets, sources, cotangent, basis_major, m2l_ops.transpose(1, 2, 0)
    )
    returned = lax.all_to_all(back, ("dx", "dy"), split_axis=0, concat_axis=0, tiled=True)
    mult, local_part, own, atoms, pairs = call_beside(
        leaf_count, targets, sources, fill, charges, cotangent, basis_major, ops
    )
    outgoing, asked = call_pack(mult, returned)
    incoming = lax.all_to_all(outgoing, ("dx", "dy"), split_axis=0, concat_axis=0, tiled=True)
    charge_grad = call_charge(asked, returned, own, atoms)
    potential = call_far(pairs, incoming, local_part, atoms, ops)
    return potential, charge_grad


def solution(mesh):
    in_specs = (
        P(("dx", "dy"), None, None),
        P(("dx", "dy"), None, None),
        P(("dx", "dy")),
        P(("dx", "dy"), None, None),
        P(),
        P(("dx", "dy"), None, None),
        P(("dx", "dy"), None, None),
        P(("dx", "dy"), None, None),
        P(("dx", "dy"), None),
        P(("dx", "dy"), None),
    )
    out_specs = (P(("dx", "dy"), None, None), P(("dx", "dy"), None, None))
    return jax.shard_map(local, mesh=mesh, in_specs=in_specs, out_specs=out_specs, check_vma=False)
```
